32 devices in a mesh: groups: 2 (over y), stem: 16 (over z, x, core).
Axes of the slice: x: 2, y: 2, z: 4, core: 2. Of those that a mesh axis runs over, the one named last changes fastest.
Arguments:
- stems: float32 [2, 2, 2097152], P('groups', None, 'stem'), parts along dimension 0, may hold values from -6 to 6
- lo_table: float32 [3, 2, 2, 256, 256], replicated, may hold values from -0.25 to 0.25
- hi_table: float32 [3, 2, 256, 256], replicated, may hold values from -0.25 to 0.25
- slice_bits: int32 [2, 3], P('groups'), parts along dimension 0, may hold values from 0 to 1
Outputs:
- window: float32 [2, 4194304], P(None, ('groups', 'stem')), parts along dimension 1
The draws below stay inside these ranges and needn't reach their ends.
There are 2 independent parts, one for each index of `groups`. The reference program is written for one: setup_inputs(seed, part) draws one part's arguments, and reference() takes and returns one part's arrays. A program takes and returns all parts, laid end to end along the dimension named above; an argument that names none is the same for every part. Nothing has to cross between parts.
Inputs may be any that keep to these rules, and one draw needn't show every extreme that they name: `slice_bits`: each entry is the value of a sliced bond of two values.
All inputs are finite; a program needn't handle non-finite values.
Results may differ from the reference program's by a relative error of at most 0.00011.
Values sent between devices are 32-bit elements; how exact they have to be, the bound alone decides.
No kernel may reach another device: no remote copies, remote signals or barrier semaphores. Data moves between devices by JAX's collectives and lax.ppermute only.
A program may use at most 64 MiB of HBM per device.

```python
import jax
import jax.numpy as jnp
from jax import lax

SLICES = 1
SPARE = 2
HI = 256
LO = 256
SEGS = 3
LEAD = 16
UNDER = 16
AMPS = 2097152


def level_of(own_key, dims, pieces, smallest, top_value):
    gain = 1.0
    for axis_at, parts in pieces:
        draws = jax.random.uniform(jax.random.fold_in(jax.random.fold_in(own_key, 6), axis_at), (parts,), jnp.float32, smallest / len(pieces), top_value / len(pieces))
        gain = gain * jnp.repeat(jnp.exp(draws), dims[axis_at] // parts).reshape((-1,) + (1,) * (len(dims) - 1 - axis_at))
    return gain


def gaussian(key, shape, width, most, shards=(), held_as=jnp.bfloat16):
    result = jax.random.normal(key, shape, jnp.float32) * width
    if len(shards) > 0:
        result = level_of(key, shape, shards, -0.22, 0.18) * result
    return jnp.clip(result, min=-most, max=most).astype(held_as)


def setup_inputs(seed: int = 0, part: int = 0) -> dict:
    key_list = jax.random.split(jax.random.key(seed), 5)
    part_keys = jax.random.split(jax.random.fold_in(key_list[4], part), 5)
    stems = gaussian(part_keys[0], (SLICES, 2, AMPS), 1.0, 6.0, ((2, 16),), jnp.float32)
    lo_table = gaussian(key_list[1], (SEGS, 2, 2, LO, LO), (2 * LO) ** -0.5, 0.25, (), jnp.float32)
    hi_table = gaussian(key_list[2], (SEGS, 2, HI, HI), (2 * HI) ** -0.5, 0.25, (), jnp.float32)
    slice_bits = jax.random.randint(part_keys[3], (SLICES, SEGS), 0, 2).astype(jnp.int32)
    return dict(stems=stems, lo_table=lo_table, hi_table=hi_table, slice_bits=slice_bits)


def complex_block(matrices):
    real_part = matrices[..., 0, :, :]
    imag_part = matrices[..., 1, :, :]
    upper_rows = jnp.stack([real_part, -imag_part], axis=-3)
    lower_rows = jnp.stack([imag_part, real_part], axis=-3)
    return jnp.stack([upper_rows, lower_rows], axis=-4)


def select_low(lo_table, slice_bits, segment):
    chosen = slice_bits[:, segment] == 1
    return jnp.where(chosen[:, None, None, None], lo_table[segment, 1][None], lo_table[segment, 0][None])


def reference(stems, lo_table, hi_table, slice_bits):
    highest = lax.Precision.HIGHEST
    low_blocks = [complex_block(select_low(lo_table, slice_bits, segment)) for segment in range(3)]
    opening = complex_block(hi_table[0])
    middle = complex_block(hi_table[1]).reshape(2, 2, LEAD, UNDER, LEAD, UNDER)
    closing = complex_block(hi_table[2])
    combined = jnp.zeros((2, LEAD, SPARE, HI, LO), jnp.float32)
    for slice_index in range(SLICES):
        amplitudes = stems[slice_index].reshape(2, LEAD, SPARE, HI, LO)
        amplitudes = jnp.einsum("carhm,dckm->darhk", amplitudes, low_blocks[0][slice_index], precision=highest)
        amplitudes = jnp.einsum("carjl,dchj->darhl", amplitudes, opening, precision=highest)
        amplitudes = jnp.einsum("carhm,dckm->darhk", amplitudes, low_blocks[1][slice_index], precision=highest)
        shaped = amplitudes.reshape(2, LEAD, SPARE, LEAD, UNDER, LO)
        amplitudes = jnp.einsum("cbrgwl,dcaubw->dargul", shaped, middle, precision=highest)
        amplitudes = amplitudes.reshape(2, LEAD, SPARE, HI, LO)
        amplitudes = jnp.einsum("carhm,dckm->darhk", amplitudes, low_blocks[2][slice_index], precision=highest)
        amplitudes = jnp.einsum("carjl,dchj->darhl", amplitudes, closing, precision=highest)
        combined = combined + amplitudes
    return combined.reshape(2, AMPS)
```

```python
import functools

import jax
import jax.numpy as jnp
from jax import lax
from jax.experimental import pallas as pl
from jax.experimental.pallas import tpu as pltpu
from jax.sharding import PartitionSpec as P

LANES = 128
SUBLANES = 8


def halves(values):
    upper = values.astype(jnp.bfloat16)
    return upper, (values - upper.astype(jnp.float32)).astype(jnp.bfloat16)


def dot_halves(left, right):
    dot = functools.partial(jnp.dot, preferred_element_type=jnp.float32)
    small = dot(left[0], right[1]) + dot(left[1], right[0])
    return dot(left[0], right[0]) + small


def complex_left(matrix, real_part, imag_part):
    width = real_part.shape[1]
    both = halves(jnp.concatenate([real_part, imag_part], axis=1))
    by_real = dot_halves(halves(matrix[0]), both)
    by_imag = dot_halves(halves(matrix[1]), both)
    return (
        by_real[:, :width] - by_imag[:, width:],
        by_real[:, width:] + by_imag[:, :width],
    )


def complex_right(real_part, imag_part, matrix):
    height = real_part.shape[0]
    both = halves(jnp.concatenate([real_part, imag_part], axis=0))
    by_real = dot_halves(both, halves(matrix[0]))
    by_imag = dot_halves(both, halves(matrix[1]))
    return (
        by_real[:height] - by_imag[height:],
        by_real[height:] + by_imag[:height],
    )


def open_kernel(stem_ref, high_ref, out_ref):
    leading, _, _, under, low = out_ref.shape
    high = leading * under
    tiles = low // LANES
    parts = [
        jnp.concatenate(
            [stem_ref[pl.ds(2 * t + c, high, stride=2 * tiles), :] for t in range(tiles)], axis=1
        )
        for c in range(2)
    ]
    for c, value in enumerate(complex_left(high_ref[0], *parts)):
        out_ref[:, 0, c] = value.reshape(leading, under, low)


def chain_kernel(bits_ref, table_ref, out_ref, held, sems):
    segments = held.shape[0]
    copies = []
    for k in range(segments):
        entry = jnp.where(bits_ref[0, k] == 1, 1, 0)
        copies.append(pltpu.make_async_copy(table_ref.at[k, entry], held.at[k], sems.at[k]))
        copies[-1].start()
    for copy in copies:
        copy.wait()
    total = (held[0, 0], held[0, 1])
    for k in range(1, segments):
        total = complex_left(held[k], *total)
    for c in range(2):
        out_ref[c] = total[c].T


def middle_kernel(in_ref, high_ref, low_ref, out_ref):
    leading, _, _, under, low = in_ref.shape
    high = leading * under
    parts = [in_ref[:, 0, c].reshape(high, low) for c in range(2)]
    parts = complex_left(high_ref[0], *parts)
    for c, value in enumerate(complex_right(*parts, low_ref)):
        out_ref[:, 0, c] = value.reshape(leading, under, low)


def close_kernel(in_ref, high_ref, out_ref):
    leading, _, _, under, low = in_ref.shape
    high = leading * under
    tiles = low // LANES
    parts = [in_ref[:, 0, c].reshape(high, low) for c in range(2)]
    for c, value in enumerate(complex_left(high_ref[0], *parts)):
        for t in range(tiles):
            out_ref[pl.ds(2 * t + c, high, stride=2 * tiles), :] = value[
                :, t * LANES : (t + 1) * LANES
            ]


def one_slice(stem, bits, lo_table, hi_table):
    leading = lax.axis_size("stem")
    segments, _, high, _ = hi_table.shape
    low = lo_table.shape[-1]
    spare = stem.shape[1] // (high * low)
    under = high // leading
    direct = under % SUBLANES == 0
    kept = (leading, under) if direct else (1, high)
    rows = high * 2 * (low // LANES)
    split_shape = (kept[0], spare, 2, kept[1], low)
    split_spec = pl.BlockSpec((kept[0], 1, 2, kept[1], low), lambda r: (0, r, 0, 0, 0))
    split_type = jax.ShapeDtypeStruct(split_shape, jnp.float32)
    stem_spec = pl.BlockSpec((rows, LANES), lambda r: (r, 0))
    flops = 2 * 4 * 3 * spare * high * high * low
    moved = 4 * stem.size * 2
    cost = pl.CostEstimate(flops=flops, bytes_accessed=moved, transcendentals=0)

    def high_spec(segment):
        return pl.BlockSpec((1, 2, high, high), lambda r: (segment, 0, 0, 0))

    def exchange(values):
        if not direct:
            values = values.reshape(spare, 2, leading, under, low).transpose(2, 0, 1, 3, 4)
        values = lax.all_to_all(values, "stem", split_axis=0, concat_axis=0, tiled=True)
        if not direct:
            values = values.transpose(1, 2, 0, 3, 4).reshape(split_shape)
        return values

    laid = stem.reshape(2, stem.shape[1] // LANES, LANES).transpose(1, 0, 2).reshape(-1, LANES)
    chain = pl.pallas_call(
        chain_kernel,
        out_shape=jax.ShapeDtypeStruct((2, low, low), jnp.float32),
        in_specs=[pl.BlockSpec(memory_space=pltpu.SMEM), pl.BlockSpec(memory_space=pl.ANY)],
        scratch_shapes=[
            pltpu.VMEM((segments, 2, low, low), jnp.float32),
            pltpu.SemaphoreType.DMA((segments,)),
        ],
        cost_estimate=cost,
        name="low_chain",
    )(bits, lo_table)
    opened = pl.pallas_call(
        open_kernel,
        grid=(spare,),
        out_shape=split_type,
        in_specs=[stem_spec, high_spec(0)],
        out_specs=split_spec,
        cost_estimate=cost,
        name="open_high",
    )(laid, hi_table)
    middle = pl.pallas_call(
        middle_kernel,
        grid=(spare,),
        out_shape=split_type,
        in_specs=[split_spec, high_spec(1), pl.BlockSpec((2, low, low), lambda r: (0, 0, 0))],
        out_specs=split_spec,
        cost_estimate=cost,
        name="middle_high_low",
    )(exchange(opened), hi_table, chain)
    closed = pl.pallas_call(
        close_kernel,
        grid=(spare,),
        out_shape=jax.ShapeDtypeStruct(laid.shape, jnp.float32),
        in_specs=[split_spec, high_spec(2)],
        out_specs=stem_spec,
        cost_estimate=cost,
        name="close_high",
    )(exchange(middle), hi_table)
    return closed.reshape(-1, 2, LANES).transpose(1, 0, 2).reshape(stem.shape)


def body(stems, lo_table, hi_table, slice_bits):
    slices = [
        one_slice(stems[s], slice_bits[s : s + 1], lo_table, hi_table)
        for s in range(stems.shape[0])
    ]
    return functools.reduce(jnp.add, slices)


def solution(mesh):
    placed = (P("groups", None, "stem"), P(), P(), P("groups", None))
    return jax.shard_map(
        body, mesh=mesh, in_specs=placed, out_specs=P(None, ("groups", "stem")), check_vma=False
    )
```

```python
import jax
import jax.numpy as jnp
from jax import lax
from jax.experimental import pallas as pl
from jax.experimental.pallas import tpu as pltpu
from jax.sharding import PartitionSpec as P

LANES = 128
SUBLANES = 8
VMEM = pl.BlockSpec(memory_space=pltpu.VMEM)
SMEM = pl.BlockSpec(memory_space=pltpu.SMEM)
HBM = pl.BlockSpec(memory_space=pltpu.HBM)
SMALL = pltpu.CompilerParams(vmem_limit_bytes=20 * 1024 * 1024)
LARGE = pltpu.CompilerParams(vmem_limit_bytes=56 * 1024 * 1024)


def halves(values):
    upper = values.astype(jnp.bfloat16)
    return upper, (values - upper.astype(jnp.float32)).astype(jnp.bfloat16)


def dot_halves(left, right):
    return jnp.dot(
        jnp.concatenate([left[0], left[0], left[1]], axis=1),
        jnp.concatenate([right[0], right[1], right[0]], axis=0),
        preferred_element_type=jnp.float32,
    )


def left_block(real_part, imag_part):
    upper = jnp.concatenate([real_part, -imag_part], axis=1)
    lower = jnp.concatenate([imag_part, real_part], axis=1)
    return jnp.concatenate([upper, lower], axis=0)


def right_block(real_part, imag_part):
    upper = jnp.concatenate([real_part, imag_part], axis=1)
    lower = jnp.concatenate([-imag_part, real_part], axis=1)
    return jnp.concatenate([upper, lower], axis=0)


def read_stem(stem_ref, high):
    tiles = stem_ref.shape[0] // (2 * high)
    parts = [
        jnp.concatenate(
            [stem_ref[pl.ds(2 * t + c, high, stride=2 * tiles), :] for t in range(tiles)], axis=1
        )
        for c in range(2)
    ]
    return jnp.concatenate(parts, axis=0)


def write_stem(stem_ref, value, high):
    tiles = stem_ref.shape[0] // (2 * high)
    for c in range(2):
        for t in range(tiles):
            stem_ref[pl.ds(2 * t + c, high, stride=2 * tiles), :] = value[
                c * high : (c + 1) * high, t * LANES : (t + 1) * LANES
            ]


def open_kernel(stem_ref, high_ref, out_ref, stem, table, sems):
    leading, spare, _, under, low = out_ref.shape
    high = leading * under
    table_copy = pltpu.make_async_copy(high_ref.at[0], table, sems.at[spare])
    table_copy.start()
    copies = [
        pltpu.make_async_copy(stem_ref.at[r], stem.at[r], sems.at[r]) for r in range(spare)
    ]
    for copy in copies:
        copy.start()
    table_copy.wait()
    matrix = halves(left_block(table[0], table[1]))
    for r in range(spare):
        copies[r].wait()
        value = dot_halves(matrix, halves(read_stem(stem.at[r], high)))
        for c in range(2):
            out_ref[:, r, c] = value[c * high : (c + 1) * high].reshape(leading, under, low)


def chain_kernel(bits_ref, table_ref, out_ref, held, sems):
    segments = held.shape[0]
    copies = []
    for k in range(segments):
        entry = jnp.where(bits_ref[0, k] == 1, 1, 0)
        copies.append(pltpu.make_async_copy(table_ref.at[k, entry], held.at[k], sems.at[k]))
        copies[-1].start()
    for copy in copies:
        copy.wait()
    low = held.shape[-1]
    total = jnp.concatenate([held[0, 0], held[0, 1]], axis=0)
    for k in range(1, segments):
        total = dot_halves(halves(left_block(held[k, 0], held[k, 1])), halves(total))
    for c in range(2):
        out_ref[c] = total[c * low : (c + 1) * low].T


def middle_kernel(in_ref, high_ref, low_ref, out_ref, high_table, low_table, sems):
    leading, spare, _, under, low = in_ref.shape
    high = leading * under
    high_copy = pltpu.make_async_copy(high_ref.at[1], high_table, sems.at[0])
    low_copy = pltpu.make_async_copy(low_ref, low_table, sems.at[1])
    high_copy.start()
    low_copy.start()
    parts = [
        halves(jnp.concatenate([in_ref[:, r, c].reshape(high, low) for c in range(2)], axis=0))
        for r in range(spare)
    ]
    high_copy.wait()
    matrix = halves(left_block(high_table[0], high_table[1]))
    parts = [dot_halves(matrix, part) for part in parts]
    low_copy.wait()
    matrix = halves(right_block(low_table[0], low_table[1]))
    for r in range(spare):
        value = jnp.concatenate([parts[r][:high], parts[r][high:]], axis=1)
        value = dot_halves(halves(value), matrix)
        for c in range(2):
            out_ref[:, r, c] = value[:, c * low : (c + 1) * low].reshape(leading, under, low)


def close_kernel(in_ref, high_ref, out_ref, held, table, sems):
    leading, spare, _, under, low = in_ref.shape
    high = leading * under
    table_copy = pltpu.make_async_copy(high_ref.at[2], table, sems.at[spare])
    table_copy.start()
    parts = [
        halves(jnp.concatenate([in_ref[:, r, c].reshape(high, low) for c in range(2)], axis=0))
        for r in range(spare)
    ]
    table_copy.wait()
    matrix = halves(left_block(table[0], table[1]))
    copies = []
    for r in range(spare):
        write_stem(held.at[r], dot_halves(matrix, parts[r]), high)
        copies.append(pltpu.make_async_copy(held.at[r], out_ref.at[r], sems.at[r]))
        copies[-1].start()
    for copy in copies:
        copy.wait()


def one_slice(stem, bits, lo_table, hi_table):
    leading = lax.axis_size("stem")
    segments, _, high, _ = hi_table.shape
    low = lo_table.shape[-1]
    rows = high * 2 * (low // LANES)
    spare = stem.size // (rows * LANES)
    under = high // leading
    direct = under % SUBLANES == 0
    kept = (leading, under) if direct else (1, high)
    split_shape = (kept[0], spare, 2, kept[1], low)
    split_type = jax.ShapeDtypeStruct(split_shape, jnp.float32)
    stem_type = jax.ShapeDtypeStruct((spare, rows, LANES), jnp.float32)
    stem_scratch = pltpu.VMEM(stem_type.shape, jnp.float32)

    def exchange(values):
        if not direct:
            values = values.reshape(spare, 2, leading, under, low).transpose(2, 0, 1, 3, 4)
        values = lax.all_to_all(values, "stem", split_axis=0, concat_axis=0, tiled=True)
        if not direct:
            values = values.transpose(1, 2, 0, 3, 4).reshape(split_shape)
        return values

    laid = stem.reshape(2, stem.shape[1] // LANES, LANES).transpose(1, 0, 2)
    laid = laid.reshape(stem_type.shape)
    table_scratch = pltpu.VMEM((2, high, high), jnp.float32)
    opened = pl.pallas_call(
        open_kernel,
        out_shape=split_type,
        in_specs=[HBM, HBM],
        out_specs=VMEM,
        scratch_shapes=[stem_scratch, table_scratch, pltpu.SemaphoreType.DMA((spare + 1,))],
        compiler_params=LARGE,
        name="open_high",
    )(laid, hi_table)
    chain = pl.pallas_call(
        chain_kernel,
        out_shape=jax.ShapeDtypeStruct((2, low, low), jnp.float32),
        in_specs=[SMEM, HBM],
        out_specs=VMEM,
        scratch_shapes=[
            pltpu.VMEM((segments, 2, low, low), jnp.float32),
            pltpu.SemaphoreType.DMA((segments,)),
        ],
        compiler_params=LARGE,
        name="low_chain",
    )(bits, lo_table)
    middle = pl.pallas_call(
        middle_kernel,
        out_shape=split_type,
        in_specs=[VMEM, HBM, HBM],
        out_specs=VMEM,
        scratch_shapes=[
            table_scratch,
            pltpu.VMEM((2, low, low), jnp.float32),
            pltpu.SemaphoreType.DMA((2,)),
        ],
        compiler_params=SMALL,
        name="middle_high_low",
    )(exchange(opened), hi_table, chain)
    closed = pl.pallas_call(
        close_kernel,
        out_shape=stem_type,
        in_specs=[VMEM, HBM],
        out_specs=HBM,
        scratch_shapes=[stem_scratch, table_scratch, pltpu.SemaphoreType.DMA((spare + 1,))],
        compiler_params=SMALL,
        name="close_high",
    )(exchange(middle), hi_table)
    return closed.reshape(-1, 2, LANES).transpose(1, 0, 2).reshape(stem.shape)


def body(stems, lo_table, hi_table, slice_bits):
    total = one_slice(stems[0], slice_bits[:1], lo_table, hi_table)
    for s in range(1, stems.shape[0]):
        total = total + one_slice(stems[s], slice_bits[s : s + 1], lo_table, hi_table)
    return total


def solution(mesh):
    placed = (P("groups", None, "stem"), P(), P(), P("groups", None))
    return jax.shard_map(
        body, mesh=mesh, in_specs=placed, out_specs=P(None, ("groups", "stem")), check_vma=False
    )
```

```python
import functools

import jax
import jax.numpy as jnp
from jax import lax
from jax.experimental import pallas as pl
from jax.experimental.pallas import tpu as pltpu
from jax.sharding import PartitionSpec as P

LANES = 128
SUBLANES = 8
VMEM = pl.BlockSpec(memory_space=pltpu.VMEM)
SMEM = pl.BlockSpec(memory_space=pltpu.SMEM)
HBM = pl.BlockSpec(memory_space=pltpu.HBM)
SMALL = pltpu.CompilerParams(vmem_limit_bytes=20 * 1024 * 1024)
LARGE = pltpu.CompilerParams(vmem_limit_bytes=56 * 1024 * 1024)


def halves(values):
    upper = values.astype(jnp.bfloat16)
    return upper, (values - upper.astype(jnp.float32)).astype(jnp.bfloat16)


def dot_halves(left, right):
    return jnp.dot(
        jnp.concatenate([left[0], left[0], left[1]], axis=1),
        jnp.concatenate([right[0], right[1], right[0]], axis=0),
        preferred_element_type=jnp.float32,
    )


def left_block(real_part, imag_part):
    upper = jnp.concatenate([real_part, -imag_part], axis=1)
    lower = jnp.concatenate([imag_part, real_part], axis=1)
    return jnp.concatenate([upper, lower], axis=0)


def right_block(real_part, imag_part):
    upper = jnp.concatenate([real_part, imag_part], axis=1)
    lower = jnp.concatenate([-imag_part, real_part], axis=1)
    return jnp.concatenate([upper, lower], axis=0)


def read_stem(stem_ref, high):
    tiles = stem_ref.shape[0] // (2 * high)
    parts = [
        jnp.concatenate(
            [stem_ref[pl.ds(2 * t + c, high, stride=2 * tiles), :] for t in range(tiles)], axis=1
        )
        for c in range(2)
    ]
    return jnp.concatenate(parts, axis=0)


def write_stem(stem_ref, value, high):
    tiles = stem_ref.shape[0] // (2 * high)
    for c in range(2):
        for t in range(tiles):
            stem_ref[pl.ds(2 * t + c, high, stride=2 * tiles), :] = value[
                c * high : (c + 1) * high, t * LANES : (t + 1) * LANES
            ]


def open_kernel(stem_ref, high_ref, out_ref, stem, table, sems):
    leading, spare, _, under, low = out_ref.shape
    high = leading * under
    table_copy = pltpu.make_async_copy(high_ref.at[0], table, sems.at[spare])
    table_copy.start()
    copies = [
        pltpu.make_async_copy(stem_ref.at[r], stem.at[r], sems.at[r]) for r in range(spare)
    ]
    for copy in copies:
        copy.start()
    table_copy.wait()
    matrix = halves(left_block(table[0], table[1]))
    for r in range(spare):
        copies[r].wait()
        value = dot_halves(matrix, halves(read_stem(stem.at[r], high)))
        for c in range(2):
            out_ref[:, r, c] = value[c * high : (c + 1) * high].reshape(leading, under, low)


def chain_kernel(bits_ref, table_ref, out_ref, held, sems):
    segments = held.shape[0]
    copies = []
    for k in range(segments):
        entry = jnp.where(bits_ref[0, k] == 1, 1, 0)
        copies.append(pltpu.make_async_copy(table_ref.at[k, entry], held.at[k], sems.at[k]))
        copies[-1].start()
    for copy in copies:
        copy.wait()
    low = held.shape[-1]
    total = jnp.concatenate([held[0, 0], held[0, 1]], axis=0)
    for k in range(1, segments):
        total = dot_halves(halves(left_block(held[k, 0], held[k, 1])), halves(total))
    for c in range(2):
        out_ref[c] = total[c * low : (c + 1) * low].T


def middle_kernel(in_ref, high_ref, low_ref, out_ref, high_table, low_table, sems):
    leading, spare, _, under, low = in_ref.shape
    high = leading * under
    high_copy = pltpu.make_async_copy(high_ref.at[1], high_table, sems.at[0])
    low_copy = pltpu.make_async_copy(low_ref, low_table, sems.at[1])
    high_copy.start()
    low_copy.start()
    parts = [
        halves(jnp.concatenate([in_ref[:, r, c].reshape(high, low) for c in range(2)], axis=0))
        for r in range(spare)
    ]
    high_copy.wait()
    matrix = halves(left_block(high_table[0], high_table[1]))
    parts = [dot_halves(matrix, part) for part in parts]
    low_copy.wait()
    matrix = halves(right_block(low_table[0], low_table[1]))
    for r in range(spare):
        value = jnp.concatenate([parts[r][:high], parts[r][high:]], axis=1)
        value = dot_halves(halves(value), matrix)
        for c in range(2):
            out_ref[:, r, c] = value[:, c * low : (c + 1) * low].reshape(leading, under, low)


def close_kernel(in_ref, high_ref, out_ref, held, table, sems):
    leading, spare, _, under, low = in_ref.shape
    high = leading * under
    table_copy = pltpu.make_async_copy(high_ref.at[2], table, sems.at[spare])
    table_copy.start()
    parts = [
        halves(jnp.concatenate([in_ref[:, r, c].reshape(high, low) for c in range(2)], axis=0))
        for r in range(spare)
    ]
    table_copy.wait()
    matrix = halves(left_block(table[0], table[1]))
    copies = []
    for r in range(spare):
        write_stem(held.at[r], dot_halves(matrix, parts[r]), high)
        copies.append(pltpu.make_async_copy(held.at[r], out_ref.at[r], sems.at[r]))
        copies[-1].start()
    for copy in copies:
        copy.wait()


def upper_order(width):
    return [0] + sorted(range(1, width), key=lambda t: (t.bit_count(), -t))


def lower_order(width):
    return [0] + sorted(range(1, width), key=lambda t: (-t.bit_length(), t))


def distances(lists, first_is_upper):
    width = len(lists)
    orders = upper_order(width), lower_order(width)
    outer, inner = orders if first_is_upper else orders[::-1]
    for n, ref in zip(outer, lists):
        for at, m in enumerate(inner):
            yield ref, at, (n * width + m if first_is_upper else m * width + n)


def rows_by_distance(table, me, under):
    devices = table.shape[1] // under
    starts = [pl.multiple_of((me ^ d) * under, under) for d in range(devices)]
    return [jnp.concatenate([table[c, pl.ds(at, under), :] for at in starts]) for c in range(2)]


def gather(in_refs, held, me, first_is_upper):
    under = in_refs[0].shape[2]
    for ref, m, distance in distances(in_refs, first_is_upper):
        at = pl.ds(pl.multiple_of((me ^ distance) * under, under), under)
        for c in range(2):
            held[c, at, :] = ref[m, c]
    return halves(jnp.concatenate([held[0], held[1]], axis=0))


def open_chunk_kernel(r, upper, me_ref, stem_ref, high_ref, *refs):
    *out_refs, stem, table, sems = refs
    under = out_refs[0].shape[2]
    stem_copy = pltpu.make_async_copy(stem_ref.at[r], stem, sems.at[0])
    table_copy = pltpu.make_async_copy(high_ref.at[0], table, sems.at[1])
    table_copy.start()
    stem_copy.start()
    table_copy.wait()
    high = table.shape[-1]
    matrix = halves(left_block(*rows_by_distance(table, me_ref[0], under)))
    stem_copy.wait()
    value = dot_halves(matrix, halves(read_stem(stem, high)))
    for ref, m, distance in distances(out_refs, upper):
        for c in range(2):
            start = c * high + distance * under
            ref[m, c] = value[start : start + under]


def turn_kernel(*refs):
    half = len(refs) // 2
    for n, in_ref in enumerate(refs[:half]):
        for m, out_ref in enumerate(refs[half:]):
            out_ref[n] = in_ref[m]


def middle_chunk_kernel(in_upper, out_upper, me_ref, high_ref, low_ref, *refs):
    *blocks, held, high_table, low_table, sems = refs
    in_refs, out_refs = blocks[: len(blocks) // 2], blocks[len(blocks) // 2 :]
    _, _, under, low = in_refs[0].shape
    high = high_table.shape[-1]
    high_copy = pltpu.make_async_copy(high_ref.at[1], high_table, sems.at[0])
    low_copy = pltpu.make_async_copy(low_ref, low_table, sems.at[1])
    high_copy.start()
    low_copy.start()
    value = gather(in_refs, held, me_ref[0], in_upper)
    high_copy.wait()
    matrix = halves(left_block(*rows_by_distance(high_table, me_ref[0], under)))
    value = dot_halves(matrix, value)
    value = jnp.concatenate([value[:high], value[high:]], axis=1)
    low_copy.wait()
    value = dot_halves(halves(value), halves(right_block(low_table[0], low_table[1])))
    for ref, m, distance in distances(out_refs, out_upper):
        for c in range(2):
            ref[m, c] = value[distance * under : (distance + 1) * under, c * low : (c + 1) * low]


def close_chunk_kernel(r, upper, width, me_ref, high_ref, *refs):
    in_refs = refs[:width]
    out_ref, held, stem, table, sems = refs[-5:]
    table_copy = pltpu.make_async_copy(high_ref.at[2], table, sems.at[0])
    table_copy.start()
    value = gather(in_refs, held, me_ref[0], upper)
    table_copy.wait()
    matrix = halves(left_block(table[0], table[1]))
    write_stem(stem, dot_halves(matrix, value), table.shape[-1])
    copy = pltpu.make_async_copy(stem, out_ref.at[r], sems.at[1])
    copy.start()
    copy.wait()


def chunks_by_permutes(laid, chain, hi_table):
    devices = lax.axis_size("stem")
    width = 1 << ((devices.bit_length() - 1) // 2)
    spare, rows, _ = laid.shape
    high, low = hi_table.shape[-1], chain.shape[-1]
    under = high // devices
    me = lax.axis_index("stem").reshape(1)
    block = jax.ShapeDtypeStruct((width, 2, under, low), jnp.float32)
    blocks = (block,) * width
    held = pltpu.VMEM((2, high, low), jnp.float32)
    table = pltpu.VMEM((2, high, high), jnp.float32)
    stem = pltpu.VMEM((rows, LANES), jnp.float32)
    sems = pltpu.SemaphoreType.DMA((2,))

    def tie(values, after):
        return lax.optimization_barrier((values, after))[0]

    def send(values, upper, late=None):
        step, order = (width, upper_order(width)) if upper else (1, lower_order(width))
        if late is not None:
            values = [*values[:-1], tie(values[-1], late)]
        return [values[0]] + [
            lax.ppermute(value, "stem", [(i, i ^ (t * step)) for i in range(devices)])
            for value, t in zip(values[1:], order[1:])
        ]

    def turn(values, name):
        return pl.pallas_call(
            turn_kernel,
            out_shape=blocks,
            in_specs=[VMEM] * width,
            out_specs=(VMEM,) * width,
            compiler_params=SMALL,
            name=name,
        )(*values)

    def open_chunk(r, upper, laid):
        return pl.pallas_call(
            functools.partial(open_chunk_kernel, r, upper),
            out_shape=blocks,
            in_specs=[SMEM, HBM, HBM],
            out_specs=(VMEM,) * width,
            scratch_shapes=[stem, table, sems],
            compiler_params=SMALL,
            name=f"open_{r}",
        )(me, laid, hi_table)

    def middle_chunk(r, in_upper, out_upper, values):
        return pl.pallas_call(
            functools.partial(middle_chunk_kernel, in_upper, out_upper),
            out_shape=blocks,
            in_specs=[SMEM, HBM, HBM] + [VMEM] * width,
            out_specs=(VMEM,) * width,
            scratch_shapes=[held, table, pltpu.VMEM(chain.shape, jnp.float32), sems],
            compiler_params=SMALL,
            name=f"middle_{r}",
        )(me, hi_table, chain, *values)

    def close_chunk(r, upper, values, done=None):
        return pl.pallas_call(
            functools.partial(close_chunk_kernel, r, upper, width),
            out_shape=jax.ShapeDtypeStruct(laid.shape, jnp.float32),
            in_specs=[SMEM, HBM] + [VMEM] * width + ([] if done is None else [HBM]),
            out_specs=HBM,
            scratch_shapes=[held, stem, table, sems],
            input_output_aliases={} if done is None else {2 + width: 0},
            compiler_params=SMALL,
            name=f"close_{r}",
        )(me, hi_table, *values, *([] if done is None else [done]))

    opened = open_chunk(0, True, laid)
    ahead = send(opened, True)
    behind = send(open_chunk(1, False, tie(laid, opened[0])), False, None)
    behind = turn(behind, "turn_1")
    behind = send(behind, True)
    ahead = turn(ahead, "turn_0")
    ahead = send(ahead, False, None)
    ahead = middle_chunk(0, False, True, ahead)
    ahead = send(ahead, True)
    behind = middle_chunk(1, True, False, behind)
    behind = send(behind, False, None)
    behind = turn(behind, "back_1")
    behind = send(behind, True)
    ahead = turn(ahead, "back_0")
    ahead = send(ahead, False, None)
    done = close_chunk(0, False, ahead)
    return close_chunk(1, True, behind, done)


def one_slice(stem, bits, lo_table, hi_table):
    leading = lax.axis_size("stem")
    segments, _, high, _ = hi_table.shape
    low = lo_table.shape[-1]
    rows = high * 2 * (low // LANES)
    spare = stem.size // (rows * LANES)
    under = high // leading
    direct = under % SUBLANES == 0
    kept = (leading, under) if direct else (1, high)
    split_shape = (kept[0], spare, 2, kept[1], low)
    split_type = jax.ShapeDtypeStruct(split_shape, jnp.float32)
    stem_type = jax.ShapeDtypeStruct((spare, rows, LANES), jnp.float32)
    stem_scratch = pltpu.VMEM(stem_type.shape, jnp.float32)

    def exchange(values):
        if not direct:
            values = values.reshape(spare, 2, leading, under, low).transpose(2, 0, 1, 3, 4)
        values = lax.all_to_all(values, "stem", split_axis=0, concat_axis=0, tiled=True)
        if not direct:
            values = values.transpose(1, 2, 0, 3, 4).reshape(split_shape)
        return values

    laid = stem.reshape(2, stem.shape[1] // LANES, LANES).transpose(1, 0, 2)
    laid = laid.reshape(stem_type.shape)
    chain = pl.pallas_call(
        chain_kernel,
        out_shape=jax.ShapeDtypeStruct((2, low, low), jnp.float32),
        in_specs=[SMEM, HBM],
        out_specs=VMEM,
        scratch_shapes=[
            pltpu.VMEM((segments, 2, low, low), jnp.float32),
            pltpu.SemaphoreType.DMA((segments,)),
        ],
        compiler_params=SMALL,
        name="low_chain",
    )(bits, lo_table)
    if direct and spare == 2 and 1 << (2 * ((leading.bit_length() - 1) // 2)) == leading:
        closed = chunks_by_permutes(laid, chain, hi_table)
        return closed.reshape(-1, 2, LANES).transpose(1, 0, 2).reshape(stem.shape)
    table_scratch = pltpu.VMEM((2, high, high), jnp.float32)
    opened = pl.pallas_call(
        open_kernel,
        out_shape=split_type,
        in_specs=[HBM, HBM],
        out_specs=VMEM,
        scratch_shapes=[stem_scratch, table_scratch, pltpu.SemaphoreType.DMA((spare + 1,))],
        compiler_params=LARGE,
        name="open_high",
    )(laid, hi_table)
    middle = pl.pallas_call(
        middle_kernel,
        out_shape=split_type,
        in_specs=[VMEM, HBM, HBM],
        out_specs=VMEM,
        scratch_shapes=[
            table_scratch,
            pltpu.VMEM((2, low, low), jnp.float32),
            pltpu.SemaphoreType.DMA((2,)),
        ],
        compiler_params=SMALL,
        name="middle_high_low",
    )(exchange(opened), hi_table, chain)
    closed = pl.pallas_call(
        close_kernel,
        out_shape=stem_type,
        in_specs=[VMEM, HBM],
        out_specs=HBM,
        scratch_shapes=[stem_scratch, table_scratch, pltpu.SemaphoreType.DMA((spare + 1,))],
        compiler_params=SMALL,
        name="close_high",
    )(exchange(middle), hi_table)
    return closed.reshape(-1, 2, LANES).transpose(1, 0, 2).reshape(stem.shape)


def body(stems, lo_table, hi_table, slice_bits):
    total = one_slice(stems[0], slice_bits[:1], lo_table, hi_table)
    for s in range(1, stems.shape[0]):
        total = total + one_slice(stems[s], slice_bits[s : s + 1], lo_table, hi_table)
    return total


def solution(mesh):
    placed = (P("groups", None, "stem"), P(), P(), P("groups", None))
    return jax.shard_map(
        body, mesh=mesh, in_specs=placed, out_specs=P(None, ("groups", "stem")), check_vma=False
    )
```

```python
import functools

import jax
import jax.numpy as jnp
from jax import lax
from jax.experimental import pallas as pl
from jax.experimental.pallas import tpu as pltpu
from jax.sharding import PartitionSpec as P

LANES = 128
SUBLANES = 8
VMEM = pl.BlockSpec(memory_space=pltpu.VMEM)
SMEM = pl.BlockSpec(memory_space=pltpu.SMEM)
HBM = pl.BlockSpec(memory_space=pltpu.HBM)
SMALL = pltpu.CompilerParams(vmem_limit_bytes=20 * 1024 * 1024)
LARGE = pltpu.CompilerParams(vmem_limit_bytes=56 * 1024 * 1024)


def halves(values):
    upper = values.astype(jnp.bfloat16)
    return upper, (values - upper.astype(jnp.float32)).astype(jnp.bfloat16)


def dot_halves(left, right):
    return jnp.dot(
        jnp.concatenate([left[0], left[0], left[1]], axis=1),
        jnp.concatenate([right[0], right[1], right[0]], axis=0),
        preferred_element_type=jnp.float32,
    )


def left_block(real_part, imag_part):
    upper = jnp.concatenate([real_part, -imag_part], axis=1)
    lower = jnp.concatenate([imag_part, real_part], axis=1)
    return jnp.concatenate([upper, lower], axis=0)


def right_block(real_part, imag_part):
    upper = jnp.concatenate([real_part, imag_part], axis=1)
    lower = jnp.concatenate([-imag_part, real_part], axis=1)
    return jnp.concatenate([upper, lower], axis=0)


def read_stem(stem_ref, high):
    tiles = stem_ref.shape[0] // (2 * high)
    parts = [
        jnp.concatenate(
            [stem_ref[pl.ds(2 * t + c, high, stride=2 * tiles), :] for t in range(tiles)], axis=1
        )
        for c in range(2)
    ]
    return jnp.concatenate(parts, axis=0)


def write_stem(stem_ref, value, high):
    tiles = stem_ref.shape[0] // (2 * high)
    for c in range(2):
        for t in range(tiles):
            stem_ref[pl.ds(2 * t + c, high, stride=2 * tiles), :] = value[
                c * high : (c + 1) * high, t * LANES : (t + 1) * LANES
            ]


def open_kernel(stem_ref, high_ref, out_ref, stem, table, sems):
    leading, spare, _, under, low = out_ref.shape
    high = leading * under
    table_copy = pltpu.make_async_copy(high_ref.at[0], table, sems.at[spare])
    table_copy.start()
    copies = [
        pltpu.make_async_copy(stem_ref.at[r], stem.at[r], sems.at[r]) for r in range(spare)
    ]
    for copy in copies:
        copy.start()
    table_copy.wait()
    matrix = halves(left_block(table[0], table[1]))
    for r in range(spare):
        copies[r].wait()
        value = dot_halves(matrix, halves(read_stem(stem.at[r], high)))
        for c in range(2):
            out_ref[:, r, c] = value[c * high : (c + 1) * high].reshape(leading, under, low)


def chain_kernel(bits_ref, table_ref, out_ref):
    segments, _, _, low, _ = table_ref.shape
    total = None
    for k in range(segments):
        entry = jnp.where(bits_ref[0, k] == 1, 1, 0)
        parts = table_ref[k, entry, 0], table_ref[k, entry, 1]
        if total is None:
            total = jnp.concatenate(parts, axis=0)
        else:
            total = dot_halves(halves(left_block(*parts)), halves(total))
    for c in range(2):
        out_ref[c] = total[c * low : (c + 1) * low].T


def middle_kernel(in_ref, high_ref, low_ref, out_ref, high_table, low_table, sems):
    leading, spare, _, under, low = in_ref.shape
    high = leading * under
    high_copy = pltpu.make_async_copy(high_ref.at[1], high_table, sems.at[0])
    low_copy = pltpu.make_async_copy(low_ref, low_table, sems.at[1])
    high_copy.start()
    low_copy.start()
    parts = [
        halves(jnp.concatenate([in_ref[:, r, c].reshape(high, low) for c in range(2)], axis=0))
        for r in range(spare)
    ]
    high_copy.wait()
    matrix = halves(left_block(high_table[0], high_table[1]))
    parts = [dot_halves(matrix, part) for part in parts]
    low_copy.wait()
    matrix = halves(right_block(low_table[0], low_table[1]))
    for r in range(spare):
        value = jnp.concatenate([parts[r][:high], parts[r][high:]], axis=1)
        value = dot_halves(halves(value), matrix)
        for c in range(2):
            out_ref[:, r, c] = value[:, c * low : (c + 1) * low].reshape(leading, under, low)


def close_kernel(in_ref, high_ref, out_ref, held, table, sems):
    leading, spare, _, under, low = in_ref.shape
    high = leading * under
    table_copy = pltpu.make_async_copy(high_ref.at[2], table, sems.at[spare])
    table_copy.start()
    parts = [
        halves(jnp.concatenate([in_ref[:, r, c].reshape(high, low) for c in range(2)], axis=0))
        for r in range(spare)
    ]
    table_copy.wait()
    matrix = halves(left_block(table[0], table[1]))
    copies = []
    for r in range(spare):
        write_stem(held.at[r], dot_halves(matrix, parts[r]), high)
        copies.append(pltpu.make_async_copy(held.at[r], out_ref.at[r], sems.at[r]))
        copies[-1].start()
    for copy in copies:
        copy.wait()


def upper_order(width):
    return [0, 1, 2, 3]


def lower_order(width):
    return [0, 3, 1, 2]


def distances(lists, first_is_upper):
    width = len(lists)
    orders = upper_order(width), lower_order(width)
    outer, inner = orders if first_is_upper else orders[::-1]
    for n, ref in zip(outer, lists):
        for at, m in enumerate(inner):
            yield ref, at, (n * width + m if first_is_upper else m * width + n)


def rows_by_distance(table, me, under):
    devices = table.shape[1] // under
    starts = [pl.multiple_of((me ^ d) * under, under) for d in range(devices)]
    return [jnp.concatenate([table[c, pl.ds(at, under), :] for at in starts]) for c in range(2)]


def gather(in_refs, held, me, first_is_upper):
    under = in_refs[0].shape[2]
    for ref, m, distance in distances(in_refs, first_is_upper):
        at = pl.ds(pl.multiple_of((me ^ distance) * under, under), under)
        for c in range(2):
            held[c, at, :] = ref[m, c]
    return halves(jnp.concatenate([held[0], held[1]], axis=0))


def open_chunk_kernel(upper, me_ref, stem_ref, table, *out_refs):
    under = out_refs[0].shape[2]
    high = table.shape[-1]
    matrix = halves(left_block(*rows_by_distance(table, me_ref[0], under)))
    value = dot_halves(matrix, halves(read_stem(stem_ref, high)))
    for ref, m, distance in distances(out_refs, upper):
        for c in range(2):
            start = c * high + distance * under
            ref[m, c] = value[start : start + under]


def turn_kernel(*refs):
    half = len(refs) // 2
    for n, in_ref in enumerate(refs[:half]):
        for m, out_ref in enumerate(refs[half:]):
            out_ref[n] = in_ref[m]


def middle_chunk_kernel(in_upper, out_upper, me_ref, table, low_table, *refs):
    *blocks, held = refs
    in_refs, out_refs = blocks[: len(blocks) // 2], blocks[len(blocks) // 2 :]
    _, _, under, low = in_refs[0].shape
    high = table.shape[-1]
    value = gather(in_refs, held, me_ref[0], in_upper)
    matrix = halves(left_block(*rows_by_distance(table, me_ref[0], under)))
    value = dot_halves(matrix, value)
    value = jnp.concatenate([value[:high], value[high:]], axis=1)
    value = dot_halves(halves(value), halves(right_block(low_table[0], low_table[1])))
    for ref, m, distance in distances(out_refs, out_upper):
        for c in range(2):
            ref[m, c] = value[distance * under : (distance + 1) * under, c * low : (c + 1) * low]


def close_chunk_kernel(r, upper, width, me_ref, table, *refs):
    in_refs = refs[:width]
    out_ref, held, stem, sem = refs[-4:]
    value = gather(in_refs, held, me_ref[0], upper)
    matrix = halves(left_block(table[0], table[1]))
    write_stem(stem, dot_halves(matrix, value), table.shape[-1])
    copy = pltpu.make_async_copy(stem, out_ref.at[r], sem)
    copy.start()
    copy.wait()


def chunks_by_permutes(laid, chain, hi_table):
    devices = lax.axis_size("stem")
    width = 1 << ((devices.bit_length() - 1) // 2)
    spare, rows, _ = laid.shape
    high, low = hi_table.shape[-1], chain.shape[-1]
    under = high // devices
    me = lax.axis_index("stem").reshape(1)
    block = jax.ShapeDtypeStruct((width, 2, under, low), jnp.float32)
    blocks = (block,) * width
    held = pltpu.VMEM((2, high, low), jnp.float32)
    stem = pltpu.VMEM((rows, LANES), jnp.float32)

    def tie(values, after):
        return lax.optimization_barrier((values, after))[0]

    def send(values, upper, ties=(None, None, None)):
        step, order = (width, upper_order(width)) if upper else (1, lower_order(width))
        values = [values[0]] + [
            value if t is None else tie(value, t) for value, t in zip(values[1:], ties)
        ]
        return [values[0]] + [
            lax.ppermute(value, "stem", [(i, i ^ (t * step)) for i in range(devices)])
            for value, t in zip(values[1:], order[1:])
        ]

    def tied(values, at, after):
        return [tie(v, after) if n == at and after is not None else v for n, v in enumerate(values)]

    def turn(values, name):
        return pl.pallas_call(
            turn_kernel,
            out_shape=blocks,
            in_specs=[VMEM] * width,
            out_specs=(VMEM,) * width,
            compiler_params=SMALL,
            name=name,
        )(*values)

    def open_chunk(r, upper, stem):
        return pl.pallas_call(
            functools.partial(open_chunk_kernel, upper),
            out_shape=blocks,
            in_specs=[SMEM, VMEM, VMEM],
            out_specs=(VMEM,) * width,
            compiler_params=SMALL,
            name=f"open_{r}",
        )(me, stem, hi_table[0])

    def middle_chunk(r, in_upper, out_upper, values):
        return pl.pallas_call(
            functools.partial(middle_chunk_kernel, in_upper, out_upper),
            out_shape=blocks,
            in_specs=[SMEM, VMEM, VMEM] + [VMEM] * width,
            out_specs=(VMEM,) * width,
            scratch_shapes=[held],
            compiler_params=SMALL,
            name=f"middle_{r}",
        )(me, hi_table[1], chain, *values)

    def close_chunk(r, upper, values, done=None):
        return pl.pallas_call(
            functools.partial(close_chunk_kernel, r, upper, width),
            out_shape=jax.ShapeDtypeStruct(laid.shape, jnp.float32),
            in_specs=[SMEM, VMEM] + [VMEM] * width + ([] if done is None else [HBM]),
            out_specs=HBM,
            scratch_shapes=[held, stem, pltpu.SemaphoreType.DMA],
            input_output_aliases={} if done is None else {2 + width: 0},
            compiler_params=SMALL,
            name=f"close_{r}",
        )(me, hi_table[2], *values, *([] if done is None else [done]))

    opened = open_chunk(0, True, laid[0])
    g1 = send(opened, True)
    g2 = send(open_chunk(1, False, tie(laid[1], opened[0])), False, (None, None, None))
    turn_1 = turn(tied(g2, 0, ((g1[1], g1[2],), chain)), "turn_1")
    g3 = send(turn_1, True, (None, None, None))
    turn_0 = turn(tied(g1, 0, turn_1[0]), "turn_0")
    g4 = send(turn_0, False, (None, None, None))
    mid0 = middle_chunk(0, False, True, tied(g4, 0, (g3[1], g3[2],)))
    g5 = send(mid0, True, (None, None, None))
    mid1 = middle_chunk(1, True, False, tied(g3, 0, None))
    g6 = send(mid1, False, (None, None, None))
    back_1 = turn(tied(g6, 2, (g5[1], g5[2],)), "back_1")
    g7 = send(back_1, True, (None, None, None))
    back_0 = turn(tied(g5, 0, back_1[0]), "back_0")
    g8 = send(back_0, False, (None, None, None))
    done = close_chunk(0, False, tied(g8, 0, (g7[1], g7[2],)))
    return close_chunk(1, True, g7, done)


def one_slice(stem, bits, lo_table, hi_table):
    leading = lax.axis_size("stem")
    segments, _, high, _ = hi_table.shape
    low = lo_table.shape[-1]
    rows = high * 2 * (low // LANES)
    spare = stem.size // (rows * LANES)
    under = high // leading
    direct = under % SUBLANES == 0
    kept = (leading, under) if direct else (1, high)
    split_shape = (kept[0], spare, 2, kept[1], low)
    split_type = jax.ShapeDtypeStruct(split_shape, jnp.float32)
    stem_type = jax.ShapeDtypeStruct((spare, rows, LANES), jnp.float32)
    stem_scratch = pltpu.VMEM(stem_type.shape, jnp.float32)

    def exchange(values):
        if not direct:
            values = values.reshape(spare, 2, leading, under, low).transpose(2, 0, 1, 3, 4)
        values = lax.all_to_all(values, "stem", split_axis=0, concat_axis=0, tiled=True)
        if not direct:
            values = values.transpose(1, 2, 0, 3, 4).reshape(split_shape)
        return values

    laid = stem.reshape(2, stem.shape[1] // LANES, LANES).transpose(1, 0, 2)
    laid = laid.reshape(stem_type.shape)
    chain = pl.pallas_call(
        chain_kernel,
        out_shape=jax.ShapeDtypeStruct((2, low, low), jnp.float32),
        in_specs=[SMEM, VMEM],
        out_specs=VMEM,
        compiler_params=SMALL,
        name="low_chain",
    )(bits, lo_table)
    if direct and spare == 2 and 1 << (2 * ((leading.bit_length() - 1) // 2)) == leading:
        closed = chunks_by_permutes(laid, chain, hi_table)
        return closed.reshape(-1, 2, LANES).transpose(1, 0, 2).reshape(stem.shape)
    table_scratch = pltpu.VMEM((2, high, high), jnp.float32)
    opened = pl.pallas_call(
        open_kernel,
        out_shape=split_type,
        in_specs=[HBM, HBM],
        out_specs=VMEM,
        scratch_shapes=[stem_scratch, table_scratch, pltpu.SemaphoreType.DMA((spare + 1,))],
        compiler_params=LARGE,
        name="open_high",
    )(laid, hi_table)
    middle = pl.pallas_call(
        middle_kernel,
        out_shape=split_type,
        in_specs=[VMEM, HBM, HBM],
        out_specs=VMEM,
        scratch_shapes=[
            table_scratch,
            pltpu.VMEM((2, low, low), jnp.float32),
            pltpu.SemaphoreType.DMA((2,)),
        ],
        compiler_params=SMALL,
        name="middle_high_low",
    )(exchange(opened), hi_table, chain)
    closed = pl.pallas_call(
        close_kernel,
        out_shape=stem_type,
        in_specs=[VMEM, HBM],
        out_specs=HBM,
        scratch_shapes=[stem_scratch, table_scratch, pltpu.SemaphoreType.DMA((spare + 1,))],
        compiler_params=SMALL,
        name="close_high",
    )(exchange(middle), hi_table)
    return closed.reshape(-1, 2, LANES).transpose(1, 0, 2).reshape(stem.shape)


def body(stems, lo_table, hi_table, slice_bits):
    total = one_slice(stems[0], slice_bits[:1], lo_table, hi_table)
    for s in range(1, stems.shape[0]):
        total = total + one_slice(stems[s], slice_bits[s : s + 1], lo_table, hi_table)
    return total


def solution(mesh):
    placed = (P("groups", None, "stem"), P(), P(), P("groups", None))
    return jax.shard_map(
        body, mesh=mesh, in_specs=placed, out_specs=P(None, ("groups", "stem")), check_vma=False
    )
```

```python
import functools

import jax
import jax.numpy as jnp
from jax import lax
from jax.experimental import pallas as pl
from jax.experimental.pallas import tpu as pltpu
from jax.sharding import PartitionSpec as P

LANES = 128
SUBLANES = 8
PIECES = 1
VMEM = pl.BlockSpec(memory_space=pltpu.VMEM)
SMEM = pl.BlockSpec(memory_space=pltpu.SMEM)
HBM = pl.BlockSpec(memory_space=pltpu.HBM)
SMALL = pltpu.CompilerParams(vmem_limit_bytes=20 * 1024 * 1024)
LARGE = pltpu.CompilerParams(vmem_limit_bytes=56 * 1024 * 1024)


def halves(values):
    upper = values.astype(jnp.bfloat16)
    return upper, (values - upper.astype(jnp.float32)).astype(jnp.bfloat16)


def dot_halves(left, right):
    return jnp.dot(
        jnp.concatenate([left[0], left[0], left[1]], axis=1),
        jnp.concatenate([right[0], right[1], right[0]], axis=0),
        preferred_element_type=jnp.float32,
    )


def left_block(real_part, imag_part):
    upper = jnp.concatenate([real_part, -imag_part], axis=1)
    lower = jnp.concatenate([imag_part, real_part], axis=1)
    return jnp.concatenate([upper, lower], axis=0)


def left_halves(real_part, imag_part):
    return [left_block(*parts) for parts in zip(halves(real_part), halves(imag_part))]


def times_right(value, real_part, imag_part):
    high, low = value.shape[0] // 2, value.shape[1]
    sides = [jnp.concatenate(parts, axis=1) for parts in zip(halves(real_part), halves(imag_part))]
    value = dot_halves(halves(value), sides)
    return (
        value[:high, :low] - value[high:, low:],
        value[high:, :low] + value[:high, low:],
    )


def read_stem(stem_ref, high):
    tiles = stem_ref.shape[0] // (2 * high)
    parts = [
        jnp.concatenate(
            [stem_ref[pl.ds(2 * t + c, high, stride=2 * tiles), :] for t in range(tiles)], axis=1
        )
        for c in range(2)
    ]
    return jnp.concatenate(parts, axis=0)


def write_stem(stem_ref, value, high):
    tiles = stem_ref.shape[0] // (2 * high)
    for c in range(2):
        for t in range(tiles):
            stem_ref[pl.ds(2 * t + c, high, stride=2 * tiles), :] = value[
                c * high : (c + 1) * high, t * LANES : (t + 1) * LANES
            ]


def open_kernel(stem_ref, high_ref, out_ref, stem, table, sems):
    leading, spare, _, under, low = out_ref.shape
    high = leading * under
    table_copy = pltpu.make_async_copy(high_ref.at[0], table, sems.at[spare])
    table_copy.start()
    copies = [
        pltpu.make_async_copy(stem_ref.at[r], stem.at[r], sems.at[r]) for r in range(spare)
    ]
    for copy in copies:
        copy.start()
    table_copy.wait()
    matrix = left_halves(table[0], table[1])
    for r in range(spare):
        copies[r].wait()
        value = dot_halves(matrix, halves(read_stem(stem.at[r], high)))
        for c in range(2):
            out_ref[:, r, c] = value[c * high : (c + 1) * high].reshape(leading, under, low)


def chain_kernel(bits_ref, table_ref, out_ref, total):
    segments, _, _, low, _ = table_ref.shape

    def chosen(k):
        return table_ref.at[k, jnp.where(bits_ref[0, k] == 1, 1, 0)]

    def step(k, carry):
        table = chosen(k)
        total[...] = dot_halves(left_halves(table[0], table[1]), halves(total[...]))
        return carry

    for c in range(2):
        total[c * low : (c + 1) * low] = chosen(0)[c]
    lax.fori_loop(1, segments, step, 0)
    for c in range(2):
        out_ref[c] = total[c * low : (c + 1) * low].T


def middle_kernel(in_ref, high_ref, low_ref, out_ref, high_table, low_table, sems):
    leading, spare, _, under, low = in_ref.shape
    high = leading * under
    high_copy = pltpu.make_async_copy(high_ref.at[1], high_table, sems.at[0])
    low_copy = pltpu.make_async_copy(low_ref, low_table, sems.at[1])
    high_copy.start()
    low_copy.start()
    parts = [
        halves(jnp.concatenate([in_ref[:, r, c].reshape(high, low) for c in range(2)], axis=0))
        for r in range(spare)
    ]
    high_copy.wait()
    matrix = left_halves(high_table[0], high_table[1])
    parts = [dot_halves(matrix, part) for part in parts]
    low_copy.wait()
    for r in range(spare):
        for c, part in enumerate(times_right(parts[r], low_table[0], low_table[1])):
            out_ref[:, r, c] = part.reshape(leading, under, low)


def close_kernel(in_ref, high_ref, out_ref, held, table, sems):
    leading, spare, _, under, low = in_ref.shape
    high = leading * under
    table_copy = pltpu.make_async_copy(high_ref.at[2], table, sems.at[spare])
    table_copy.start()
    parts = [
        halves(jnp.concatenate([in_ref[:, r, c].reshape(high, low) for c in range(2)], axis=0))
        for r in range(spare)
    ]
    table_copy.wait()
    matrix = left_halves(table[0], table[1])
    copies = []
    for r in range(spare):
        write_stem(held.at[r], dot_halves(matrix, parts[r]), high)
        copies.append(pltpu.make_async_copy(held.at[r], out_ref.at[r], sems.at[r]))
        copies[-1].start()
    for copy in copies:
        copy.wait()


def layout_over(values, others):
    return tuple(tuple(value + other for other in others) for value in values)


def distances(layout):
    for n, array in enumerate(layout):
        for m, distance in enumerate(array):
            yield n, m, distance


def rows_by_distance(table, me, under):
    devices = table.shape[1] // under
    starts = [pl.multiple_of((me ^ d) * under, under) for d in range(devices)]
    return [jnp.concatenate([table[c, pl.ds(at, under), :] for at in starts]) for c in range(2)]


def gather(in_refs, held, me, layout):
    under = in_refs[0].shape[2]
    for n, m, distance in distances(layout):
        at = pl.ds(pl.multiple_of((me ^ distance) * under, under), under)
        for c in range(2):
            held[c, at, :] = in_refs[n][m, c]
    return halves(jnp.concatenate([held[0], held[1]], axis=0))


def open_chunk_kernel(layout, me_ref, stem_ref, table, *out_refs):
    under = out_refs[0].shape[2]
    high = table.shape[-1]
    matrix = left_halves(*rows_by_distance(table, me_ref[0], under))
    value = dot_halves(matrix, halves(read_stem(stem_ref, high)))
    for n, m, distance in distances(layout):
        for c in range(2):
            start = c * high + distance * under
            out_refs[n][m, c] = value[start : start + under]


def turn_kernel(old, new, *refs):
    place = {distance: (n, m) for n, m, distance in distances(old)}
    for n, m, distance in distances(new):
        at = place[distance]
        refs[len(old) + n][m] = refs[at[0]][at[1]]


def middle_chunk_kernel(old, new, me_ref, table, low_table, *refs):
    *blocks, held, between = refs
    in_refs, out_refs = blocks[: len(old)], blocks[len(old) :]
    under = in_refs[0].shape[2]

    def stage(n, carry):
        @pl.when(n == 0)
        def high_modes():
            value = gather(in_refs, held, me_ref[0], old)
            matrix = left_halves(*rows_by_distance(table, me_ref[0], under))
            between[...] = dot_halves(matrix, value)

        @pl.when(n == 1)
        def low_modes():
            parts = times_right(between[...], low_table[0], low_table[1])
            for n, m, distance in distances(new):
                for c in range(2):
                    out_refs[n][m, c] = parts[c][distance * under : (distance + 1) * under]

        return carry

    lax.fori_loop(0, 2, stage, 0)


def close_chunk_kernel(r, layout, me_ref, table, *refs):
    in_refs = refs[: len(layout)]
    out_ref, held, stem, sems = refs[-4:]
    pieces = sems.shape[0]
    high, rows = table.shape[-1] // pieces, stem.shape[0] // pieces
    gather(in_refs, held, me_ref[0], layout)

    def copy(n):
        at = pl.ds(n * rows, rows)
        return pltpu.make_async_copy(stem.at[at], out_ref.at[r, at], sems.at[n])

    def piece(n, carry):
        some = pl.ds(n * high, high)
        matrix = left_halves(table[0, some], table[1, some])
        value = halves(jnp.concatenate([held[0], held[1]], axis=0))
        write_stem(stem.at[pl.ds(n * rows, rows)], dot_halves(matrix, value), high)
        copy(n).start()
        return carry

    lax.fori_loop(0, pieces, piece, 0)
    for n in range(pieces):
        copy(n).wait()


def chunks_by_permutes(laid, chain, hi_table):
    devices = lax.axis_size("stem")
    width = 1 << ((devices.bit_length() - 1) // 2)
    spare, rows, _ = laid.shape
    high, low = hi_table.shape[-1], chain.shape[-1]
    under = high // devices
    me = lax.axis_index("stem").reshape(1)
    held = pltpu.VMEM((2, high, low), jnp.float32)
    stem = pltpu.VMEM((rows, LANES), jnp.float32)

    def tie(values, after):
        return lax.optimization_barrier((values, after))[0]

    def blocks(layout):
        shapes = [(len(array), 2, under, low) for array in layout]
        return tuple(jax.ShapeDtypeStruct(shape, jnp.float32) for shape in shapes)

    def swap(value, step, after=None):
        value = value if after is None else tie(value, after)
        return lax.ppermute(value, "stem", [(i, i ^ step) for i in range(devices)])

    def tied(values, at, after):
        return [tie(v, after) if n == at else v for n, v in enumerate(values)]

    def turn(old, new, values, name):
        return pl.pallas_call(
            functools.partial(turn_kernel, old, new),
            out_shape=blocks(new),
            in_specs=[VMEM] * len(old),
            out_specs=(VMEM,) * len(new),
            compiler_params=SMALL,
            name=name,
        )(*values)

    def open_chunk(r, layout, stem):
        return pl.pallas_call(
            functools.partial(open_chunk_kernel, layout),
            out_shape=blocks(layout),
            in_specs=[SMEM, VMEM, VMEM],
            out_specs=(VMEM,) * len(layout),
            compiler_params=SMALL,
            name=f"open_{r}",
        )(me, stem, hi_table[0])

    def middle_chunk(r, old, new, values):
        return pl.pallas_call(
            functools.partial(middle_chunk_kernel, old, new),
            out_shape=blocks(new),
            in_specs=[SMEM, VMEM, VMEM] + [VMEM] * len(old),
            out_specs=(VMEM,) * len(new),
            scratch_shapes=[held, pltpu.VMEM((2 * high, low), jnp.float32)],
            compiler_params=SMALL,
            name=f"middle_{r}",
        )(me, hi_table[1], chain, *values)

    def close_chunk(r, layout, values, done=None):
        return pl.pallas_call(
            functools.partial(close_chunk_kernel, r, layout),
            out_shape=jax.ShapeDtypeStruct(laid.shape, jnp.float32),
            in_specs=[SMEM, VMEM] + [VMEM] * len(layout) + ([] if done is None else [HBM]),
            out_specs=HBM,
            scratch_shapes=[held, stem, pltpu.SemaphoreType.DMA((PIECES,))],
            input_output_aliases={} if done is None else {2 + len(layout): 0},
            compiler_params=SMALL,
            name=f"close_{r}",
        )(me, hi_table[2], *values, *([] if done is None else [done]))

    L00z = layout_over((0, 4, 8, 12), (0, 1, 3, 2))
    L00p = layout_over((0, 1, 3, 2), (0, 4, 8, 12))
    L01z = layout_over((0, 4, 8, 12), (0, 1, 3, 2))
    L01p = layout_over((0, 1, 3, 2), (0, 4, 8, 12))
    L10p = layout_over((0, 1, 3, 2), (0, 4, 8, 12))
    L10z = layout_over((0, 4, 8, 12), (0, 1, 3, 2))
    L11p = layout_over((0, 1, 3, 2), (0, 4, 8, 12))
    L11z = layout_over((0, 4, 8, 12), (0, 1, 3, 2))
    open_0 = open_chunk(0, L00z, laid[0])
    open_1 = open_chunk(1, L10p, tie(laid[1], open_0[0]))
    open_0_1 = swap(open_0[1], 4)
    open_0_2 = swap(open_0[2], 8)
    open_0_3 = swap(open_0[3], 12)
    open_1_1 = swap(open_1[1], 1)
    open_1_2 = swap(open_1[2], 3)
    open_1_3 = swap(open_1[3], 2)
    turn_101 = turn(L10p, L10z, tied([open_1[0], open_1_1, open_1_2, open_1_3], 0, (open_0_1, open_0_2, chain)), "turn_101")
    turn_001 = turn(L00z, L00p, tied([open_0[0], open_0_1, open_0_2, open_0_3], 0, turn_101[0]), "turn_001")
    turn_001_1 = swap(turn_001[1], 1)
    turn_001_2 = swap(turn_001[2], 3)
    turn_001_3 = swap(turn_001[3], 2)
    turn_101_1 = swap(turn_101[1], 4)
    turn_101_2 = swap(turn_101[2], 8)
    middle_0 = middle_chunk(0, L00p, L01z, tied([turn_001[0], turn_001_1, turn_001_2, turn_001_3], 0, (turn_101_1, turn_101_2)))
    middle_0_1 = swap(middle_0[1], 4)
    middle_0_2 = swap(middle_0[2], 8)
    middle_0_3 = swap(middle_0[3], 12)
    turn_101_3 = swap(turn_101[3], 12)
    middle_1 = middle_chunk(1, L10z, L11p, [turn_101[0], turn_101_1, turn_101_2, turn_101_3])
    middle_1_1 = swap(middle_1[1], 1)
    middle_1_2 = swap(middle_1[2], 3)
    middle_1_3 = swap(middle_1[3], 2)
    turn_111 = turn(L11p, L11z, tied([middle_1[0], middle_1_1, middle_1_2, middle_1_3], 2, (middle_0_1, middle_0_2)), "turn_111")
    turn_011 = turn(L01z, L01p, tied([middle_0[0], middle_0_1, middle_0_2, middle_0_3], 0, turn_111[0]), "turn_011")
    turn_011_1 = swap(turn_011[1], 1)
    turn_011_2 = swap(turn_011[2], 3)
    turn_011_3 = swap(turn_011[3], 2)
    turn_111_1 = swap(turn_111[1], 4)
    turn_111_2 = swap(turn_111[2], 8)
    close_0 = close_chunk(0, L01p, tied([turn_011[0], turn_011_1, turn_011_2, turn_011_3], 0, (turn_111_1, turn_111_2)))
    turn_111_3 = swap(turn_111[3], 12)
    return close_chunk(1, L11z, [turn_111[0], turn_111_1, turn_111_2, turn_111_3], close_0)


def one_slice(stem, bits, lo_table, hi_table):
    leading = lax.axis_size("stem")
    segments, _, high, _ = hi_table.shape
    low = lo_table.shape[-1]
    rows = high * 2 * (low // LANES)
    spare = stem.size // (rows * LANES)
    under = high // leading
    direct = under % SUBLANES == 0
    kept = (leading, under) if direct else (1, high)
    split_shape = (kept[0], spare, 2, kept[1], low)
    split_type = jax.ShapeDtypeStruct(split_shape, jnp.float32)
    stem_type = jax.ShapeDtypeStruct((spare, rows, LANES), jnp.float32)
    stem_scratch = pltpu.VMEM(stem_type.shape, jnp.float32)

    def exchange(values):
        if not direct:
            values = values.reshape(spare, 2, leading, under, low).transpose(2, 0, 1, 3, 4)
        values = lax.all_to_all(values, "stem", split_axis=0, concat_axis=0, tiled=True)
        if not direct:
            values = values.transpose(1, 2, 0, 3, 4).reshape(split_shape)
        return values

    laid = stem.reshape(2, stem.shape[1] // LANES, LANES).transpose(1, 0, 2)
    laid = laid.reshape(stem_type.shape)
    chain = pl.pallas_call(
        chain_kernel,
        out_shape=jax.ShapeDtypeStruct((2, low, low), jnp.float32),
        in_specs=[SMEM, VMEM],
        out_specs=VMEM,
        scratch_shapes=[pltpu.VMEM((2 * low, low), jnp.float32)],
        compiler_params=SMALL,
        name="low_chain",
    )(bits, lo_table)
    if direct and spare == 2 and 1 << (2 * ((leading.bit_length() - 1) // 2)) == leading:
        closed = chunks_by_permutes(laid, chain, hi_table)
        return closed.reshape(-1, 2, LANES).transpose(1, 0, 2).reshape(stem.shape)
    table_scratch = pltpu.VMEM((2, high, high), jnp.float32)
    opened = pl.pallas_call(
        open_kernel,
        out_shape=split_type,
        in_specs=[HBM, HBM],
        out_specs=VMEM,
        scratch_shapes=[stem_scratch, table_scratch, pltpu.SemaphoreType.DMA((spare + 1,))],
        compiler_params=LARGE,
        name="open_high",
    )(laid, hi_table)
    middle = pl.pallas_call(
        middle_kernel,
        out_shape=split_type,
        in_specs=[VMEM, HBM, HBM],
        out_specs=VMEM,
        scratch_shapes=[
            table_scratch,
            pltpu.VMEM((2, low, low), jnp.float32),
            pltpu.SemaphoreType.DMA((2,)),
        ],
        compiler_params=SMALL,
        name="middle_high_low",
    )(exchange(opened), hi_table, chain)
    closed = pl.pallas_call(
        close_kernel,
        out_shape=stem_type,
        in_specs=[VMEM, HBM],
        out_specs=HBM,
        scratch_shapes=[stem_scratch, table_scratch, pltpu.SemaphoreType.DMA((spare + 1,))],
        compiler_params=SMALL,
        name="close_high",
    )(exchange(middle), hi_table)
    return closed.reshape(-1, 2, LANES).transpose(1, 0, 2).reshape(stem.shape)


def body(stems, lo_table, hi_table, slice_bits):
    total = one_slice(stems[0], slice_bits[:1], lo_table, hi_table)
    for s in range(1, stems.shape[0]):
        total = total + one_slice(stems[s], slice_bits[s : s + 1], lo_table, hi_table)
    return total


def solution(mesh):
    placed = (P("groups", None, "stem"), P(), P(), P("groups", None))
    return jax.shard_map(
        body, mesh=mesh, in_specs=placed, out_specs=P(None, ("groups", "stem")), check_vma=False
    )
```

```python
import functools

import jax
import jax.numpy as jnp
from jax import lax
from jax.experimental import pallas as pl
from jax.experimental.pallas import tpu as pltpu
from jax.sharding import PartitionSpec as P

LANES = 128
SUBLANES = 8
VMEM = pl.BlockSpec(memory_space=pltpu.VMEM)
SMEM = pl.BlockSpec(memory_space=pltpu.SMEM)
HBM = pl.BlockSpec(memory_space=pltpu.HBM)
SMALL = pltpu.CompilerParams(vmem_limit_bytes=20 * 1024 * 1024)
LARGE = pltpu.CompilerParams(vmem_limit_bytes=56 * 1024 * 1024)


def halves(values):
    upper = values.astype(jnp.bfloat16)
    return upper, (values - upper.astype(jnp.float32)).astype(jnp.bfloat16)


def dot_halves(left, right):
    return jnp.dot(
        jnp.concatenate([left[0], left[0], left[1]], axis=1),
        jnp.concatenate([right[0], right[1], right[0]], axis=0),
        preferred_element_type=jnp.float32,
    )


def left_block(real_part, imag_part):
    upper = jnp.concatenate([real_part, -imag_part], axis=1)
    lower = jnp.concatenate([imag_part, real_part], axis=1)
    return jnp.concatenate([upper, lower], axis=0)


def left_halves(real_part, imag_part):
    return [left_block(*parts) for parts in zip(halves(real_part), halves(imag_part))]


def times_right(value, real_part, imag_part):
    high, low = value.shape[0] // 2, value.shape[1]
    sides = [jnp.concatenate(parts, axis=1) for parts in zip(halves(real_part), halves(imag_part))]
    value = dot_halves(halves(value), sides)
    return (
        value[:high, :low] - value[high:, low:],
        value[high:, :low] + value[:high, low:],
    )


def read_stem(stem_ref, high):
    tiles = stem_ref.shape[0] // (2 * high)
    parts = [
        jnp.concatenate(
            [stem_ref[pl.ds(2 * t + c, high, stride=2 * tiles), :] for t in range(tiles)], axis=1
        )
        for c in range(2)
    ]
    return jnp.concatenate(parts, axis=0)


def write_stem(stem_ref, value, high):
    tiles = stem_ref.shape[0] // (2 * high)
    for c in range(2):
        for t in range(tiles):
            stem_ref[pl.ds(2 * t + c, high, stride=2 * tiles), :] = value[
                c * high : (c + 1) * high, t * LANES : (t + 1) * LANES
            ]


def open_kernel(stem_ref, high_ref, out_ref, stem, table, sems):
    leading, spare, _, under, low = out_ref.shape
    high = leading * under
    table_copy = pltpu.make_async_copy(high_ref.at[0], table, sems.at[spare])
    table_copy.start()
    copies = [
        pltpu.make_async_copy(stem_ref.at[r], stem.at[r], sems.at[r]) for r in range(spare)
    ]
    for copy in copies:
        copy.start()
    table_copy.wait()
    matrix = left_halves(table[0], table[1])
    for r in range(spare):
        copies[r].wait()
        value = dot_halves(matrix, halves(read_stem(stem.at[r], high)))
        for c in range(2):
            out_ref[:, r, c] = value[c * high : (c + 1) * high].reshape(leading, under, low)


def chain_kernel(bits_ref, table_ref, out_ref, total):
    segments, _, _, low, _ = table_ref.shape

    def chosen(k):
        return table_ref.at[k, jnp.where(bits_ref[0, k] == 1, 1, 0)]

    def step(k, carry):
        table = chosen(k)
        total[...] = dot_halves(left_halves(table[0], table[1]), halves(total[...]))
        return carry

    for c in range(2):
        total[c * low : (c + 1) * low] = chosen(0)[c]
    lax.fori_loop(1, segments, step, 0)
    for c in range(2):
        out_ref[c] = total[c * low : (c + 1) * low].T


def middle_kernel(in_ref, high_ref, low_ref, out_ref, high_table, low_table, sems):
    leading, spare, _, under, low = in_ref.shape
    high = leading * under
    high_copy = pltpu.make_async_copy(high_ref.at[1], high_table, sems.at[0])
    low_copy = pltpu.make_async_copy(low_ref, low_table, sems.at[1])
    high_copy.start()
    low_copy.start()
    parts = [
        halves(jnp.concatenate([in_ref[:, r, c].reshape(high, low) for c in range(2)], axis=0))
        for r in range(spare)
    ]
    high_copy.wait()
    matrix = left_halves(high_table[0], high_table[1])
    parts = [dot_halves(matrix, part) for part in parts]
    low_copy.wait()
    for r in range(spare):
        for c, part in enumerate(times_right(parts[r], low_table[0], low_table[1])):
            out_ref[:, r, c] = part.reshape(leading, under, low)


def close_kernel(in_ref, high_ref, out_ref, held, table, sems):
    leading, spare, _, under, low = in_ref.shape
    high = leading * under
    table_copy = pltpu.make_async_copy(high_ref.at[2], table, sems.at[spare])
    table_copy.start()
    parts = [
        halves(jnp.concatenate([in_ref[:, r, c].reshape(high, low) for c in range(2)], axis=0))
        for r in range(spare)
    ]
    table_copy.wait()
    matrix = left_halves(table[0], table[1])
    copies = []
    for r in range(spare):
        write_stem(held.at[r], dot_halves(matrix, parts[r]), high)
        copies.append(pltpu.make_async_copy(held.at[r], out_ref.at[r], sems.at[r]))
        copies[-1].start()
    for copy in copies:
        copy.wait()


def layout_over(values, others):
    return tuple(tuple(value + other for other in others) for value in values)


def distances(layout):
    for n, array in enumerate(layout):
        for m, distance in enumerate(array):
            yield n, m, distance


def rows_by_distance(parts, me, under):
    devices = parts[0].shape[0] // under
    starts = [pl.multiple_of((me ^ d) * under, under) for d in range(devices)]
    return [
        jnp.concatenate([part[pl.ds(at, under), :] for at in starts], axis=0) for part in parts
    ]


def gather(in_refs, held, me, layout):
    under = in_refs[0].shape[2]
    for n, m, distance in distances(layout):
        at = pl.ds(pl.multiple_of((me ^ distance) * under, under), under)
        for c in range(2):
            held[c, at, :] = in_refs[n][m, c]
    return halves(jnp.concatenate([held[0], held[1]], axis=0))


def open_chunk(layout, me_ref, stem_ref, parts, out_refs):
    under = out_refs[0].shape[2]
    high = parts[0].shape[0]
    matrix = left_halves(*rows_by_distance(parts, me_ref[0], under))
    value = dot_halves(matrix, halves(read_stem(stem_ref, high)))
    for n, m, distance in distances(layout):
        for c in range(2):
            start = c * high + distance * under
            out_refs[n][m, c] = value[start : start + under]


def open_chunk_kernel(layout, me_ref, stem_ref, table, *out_refs):
    open_chunk(layout, me_ref, stem_ref, (table.at[0], table.at[1]), out_refs)


def open_first_kernel(layout, me_ref, packed_ref, *refs):
    *out_refs, table = refs
    _, high, _ = table.shape
    tiles = high // LANES
    rows = packed_ref.shape[0] - 2 * high * tiles
    matrix = packed_ref[rows:].reshape(2, high // SUBLANES, tiles, SUBLANES, LANES)
    for c in range(2):
        for t in range(tiles):
            part = matrix[c, :, t].reshape(high, LANES)
            table[c, :, t * LANES : (t + 1) * LANES] = part
    parts = table.at[0], table.at[1]
    open_chunk(layout, me_ref, packed_ref.at[pl.ds(0, rows)], parts, out_refs)


def turn_kernel(old, new, *refs):
    place = {distance: (n, m) for n, m, distance in distances(old)}
    for n, m, distance in distances(new):
        at = place[distance]
        refs[len(old) + n][m] = refs[at[0]][at[1]]


def middle_chunk_kernel(old, new, me_ref, table, low_table, *refs):
    *blocks, held, between = refs
    in_refs, out_refs = blocks[: len(old)], blocks[len(old) :]
    under = in_refs[0].shape[2]

    def stage(n, carry):
        @pl.when(n == 0)
        def high_modes():
            value = gather(in_refs, held, me_ref[0], old)
            matrix = left_halves(*rows_by_distance((table.at[0], table.at[1]), me_ref[0], under))
            between[...] = dot_halves(matrix, value)

        @pl.when(n == 1)
        def low_modes():
            parts = times_right(between[...], low_table[0], low_table[1])
            for n, m, distance in distances(new):
                for c in range(2):
                    out_refs[n][m, c] = parts[c][distance * under : (distance + 1) * under]

        return carry

    lax.fori_loop(0, 2, stage, 0)


def close_chunk(layout, me_ref, table, in_refs, held, stem):
    value = gather(in_refs, held, me_ref[0], layout)
    matrix = left_halves(table[0], table[1])
    write_stem(stem, dot_halves(matrix, value), table.shape[-1])


def close_first_kernel(layout, me_ref, table, *refs):
    *in_refs, out_ref, held = refs
    close_chunk(layout, me_ref, table, in_refs, held, out_ref)


def close_last_kernel(layout, me_ref, table, *refs):
    *in_refs, first_ref, out_ref, held, stem, sems = refs
    copies = [
        pltpu.make_async_copy(first_ref, out_ref.at[0], sems.at[0]),
        pltpu.make_async_copy(stem, out_ref.at[1], sems.at[1]),
    ]
    copies[0].start()
    close_chunk(layout, me_ref, table, in_refs, held, stem)
    copies[1].start()
    for copy in copies:
        copy.wait()


def chunks_by_permutes(laid, chain, hi_table):
    devices = lax.axis_size("stem")
    width = 1 << ((devices.bit_length() - 1) // 2)
    spare, rows, _ = laid.shape
    high, low = hi_table.shape[-1], chain.shape[-1]
    under = high // devices
    me = lax.axis_index("stem").reshape(1)
    held = pltpu.VMEM((2, high, low), jnp.float32)
    stem = pltpu.VMEM((rows, LANES), jnp.float32)

    def tie(values, after):
        return lax.optimization_barrier((values, after))[0]

    def blocks(layout):
        shapes = [(len(array), 2, under, low) for array in layout]
        return tuple(jax.ShapeDtypeStruct(shape, jnp.float32) for shape in shapes)

    def swap(value, step, after=None):
        value = value if after is None else tie(value, after)
        return lax.ppermute(value, "stem", [(i, i ^ step) for i in range(devices)])

    def tied(values, at, after):
        return [tie(v, after) if n == at else v for n, v in enumerate(values)]

    def turn(old, new, values, name):
        return pl.pallas_call(
            functools.partial(turn_kernel, old, new),
            out_shape=blocks(new),
            in_specs=[VMEM] * len(old),
            out_specs=(VMEM,) * len(new),
            compiler_params=SMALL,
            name=name,
        )(*values)

    def open_chunk_0(layout):
        tiles = high // LANES
        matrix = hi_table[0].reshape(2, high // SUBLANES, SUBLANES, tiles, LANES)
        matrix = matrix.transpose(0, 1, 3, 2, 4).reshape(-1, LANES)
        return pl.pallas_call(
            functools.partial(open_first_kernel, layout),
            out_shape=blocks(layout),
            in_specs=[SMEM, VMEM],
            out_specs=(VMEM,) * len(layout),
            scratch_shapes=[pltpu.VMEM((2, high, high), jnp.float32)],
            compiler_params=SMALL,
            name="open_0",
        )(me, jnp.concatenate([laid[0], matrix], axis=0))

    def open_chunk_1(layout, stem, table):
        return pl.pallas_call(
            functools.partial(open_chunk_kernel, layout),
            out_shape=blocks(layout),
            in_specs=[SMEM, VMEM, VMEM],
            out_specs=(VMEM,) * len(layout),
            compiler_params=SMALL,
            name="open_1",
        )(me, stem, table)

    def middle_chunk(r, old, new, values):
        return pl.pallas_call(
            functools.partial(middle_chunk_kernel, old, new),
            out_shape=blocks(new),
            in_specs=[SMEM, VMEM, VMEM] + [VMEM] * len(old),
            out_specs=(VMEM,) * len(new),
            scratch_shapes=[held, pltpu.VMEM((2 * high, low), jnp.float32)],
            compiler_params=SMALL,
            name=f"middle_{r}",
        )(me, later[1][1], chain, *values)

    def close_chunk(r, layout, values, first=None):
        if first is None:
            return pl.pallas_call(
                functools.partial(close_first_kernel, layout),
                out_shape=jax.ShapeDtypeStruct(laid.shape[1:], jnp.float32),
                in_specs=[SMEM, VMEM] + [VMEM] * len(layout),
                out_specs=VMEM,
                scratch_shapes=[held],
                compiler_params=SMALL,
                name=f"close_{r}",
            )(me, later[1][2], *values)
        return pl.pallas_call(
            functools.partial(close_last_kernel, layout),
            out_shape=jax.ShapeDtypeStruct(laid.shape, jnp.float32),
            in_specs=[SMEM, VMEM] + [VMEM] * len(layout) + [VMEM],
            out_specs=HBM,
            scratch_shapes=[held, stem, pltpu.SemaphoreType.DMA((2,))],
            compiler_params=SMALL,
            name=f"close_{r}",
        )(me, later[1][2], *values, first)

    L00z = layout_over((0, 4, 8, 12), (0, 3, 1, 2))
    L00p = layout_over((0, 3, 1, 2), (0, 4, 8, 12))
    L01z = layout_over((0, 4, 8, 12), (0, 1, 2, 3))
    L01p = layout_over((0, 1, 2, 3), (0, 4, 8, 12))
    L10p = layout_over((0, 2, 1, 3), (0, 4, 8, 12))
    L10z = layout_over((0, 4, 8, 12), (0, 2, 1, 3))
    L11p = layout_over((0, 1, 3, 2), (0, 4, 8, 12))
    L11z = layout_over((0, 4, 8, 12), (0, 1, 3, 2))
    open_0 = open_chunk_0(L00z)
    later = tie((laid, hi_table), open_0[0])
    open_1 = open_chunk_1(L10p, later[0][1], later[1][0])
    open_0_1 = swap(open_0[1], 4)
    open_0_2 = swap(open_0[2], 8)
    open_0_3 = swap(open_0[3], 12)
    turn_001 = turn(L00z, L00p, [open_0[0], open_0_1, open_0_2, open_0_3], "turn_001")
    turn_001_1 = swap(turn_001[1], 3)
    turn_001_2 = swap(turn_001[2], 1)
    turn_001_3 = swap(turn_001[3], 2)
    open_1_1 = swap(open_1[1], 2)
    open_1_2 = swap(open_1[2], 1)
    open_1_3 = swap(open_1[3], 3)
    turn_101 = turn(L10p, L10z, tied([open_1[0], open_1_1, open_1_2, open_1_3], 0, (open_0_1, open_0_2, chain)), "turn_101")
    turn_101_1 = swap(turn_101[1], 4)
    turn_101_2 = swap(turn_101[2], 8)
    middle_0 = middle_chunk(0, L00p, L01z, tied([turn_001[0], turn_001_1, turn_001_2, turn_001_3], 0, (turn_101_1, turn_101_2)))
    middle_0_1 = swap(middle_0[1], 4)
    middle_0_2 = swap(middle_0[2], 8)
    middle_0_3 = swap(middle_0[3], 12)
    turn_011 = turn(L01z, L01p, [middle_0[0], middle_0_1, middle_0_2, middle_0_3], "turn_011")
    turn_011_1 = swap(turn_011[1], 1)
    turn_011_2 = swap(turn_011[2], 2)
    turn_011_3 = swap(turn_011[3], 3)
    turn_101_3 = swap(turn_101[3], 12)
    middle_1 = middle_chunk(1, L10z, L11p, [turn_101[0], turn_101_1, turn_101_2, turn_101_3])
    middle_1_1 = swap(middle_1[1], 1)
    middle_1_2 = swap(middle_1[2], 3)
    middle_1_3 = swap(middle_1[3], 2)
    turn_111 = turn(L11p, L11z, tied([middle_1[0], middle_1_1, middle_1_2, middle_1_3], 2, (middle_0_1, middle_0_2)), "turn_111")
    turn_111_1 = swap(turn_111[1], 4)
    turn_111_2 = swap(turn_111[2], 8)
    close_0 = close_chunk(0, L01p, tied([turn_011[0], turn_011_1, turn_011_2, turn_011_3], 0, (turn_111_1, turn_111_2)))
    turn_111_3 = swap(turn_111[3], 12)
    return close_chunk(1, L11z, [turn_111[0], turn_111_1, turn_111_2, turn_111_3], close_0)


def one_slice(stem, bits, lo_table, hi_table):
    leading = lax.axis_size("stem")
    segments, _, high, _ = hi_table.shape
    low = lo_table.shape[-1]
    rows = high * 2 * (low // LANES)
    spare = stem.size // (rows * LANES)
    under = high // leading
    direct = under % SUBLANES == 0
    kept = (leading, under) if direct else (1, high)
    split_shape = (kept[0], spare, 2, kept[1], low)
    split_type = jax.ShapeDtypeStruct(split_shape, jnp.float32)
    stem_type = jax.ShapeDtypeStruct((spare, rows, LANES), jnp.float32)
    stem_scratch = pltpu.VMEM(stem_type.shape, jnp.float32)

    def exchange(values):
        if not direct:
            values = values.reshape(spare, 2, leading, under, low).transpose(2, 0, 1, 3, 4)
        values = lax.all_to_all(values, "stem", split_axis=0, concat_axis=0, tiled=True)
        if not direct:
            values = values.transpose(1, 2, 0, 3, 4).reshape(split_shape)
        return values

    laid = stem.reshape(2, stem.shape[1] // LANES, LANES).transpose(1, 0, 2)
    laid = laid.reshape(stem_type.shape)
    chain = pl.pallas_call(
        chain_kernel,
        out_shape=jax.ShapeDtypeStruct((2, low, low), jnp.float32),
        in_specs=[SMEM, VMEM],
        out_specs=VMEM,
        scratch_shapes=[pltpu.VMEM((2 * low, low), jnp.float32)],
        compiler_params=SMALL,
        name="low_chain",
    )(bits, lo_table)
    if direct and spare == 2 and 1 << (2 * ((leading.bit_length() - 1) // 2)) == leading:
        closed = chunks_by_permutes(laid, chain, hi_table)
        return closed.reshape(-1, 2, LANES).transpose(1, 0, 2).reshape(stem.shape)
    table_scratch = pltpu.VMEM((2, high, high), jnp.float32)
    opened = pl.pallas_call(
        open_kernel,
        out_shape=split_type,
        in_specs=[HBM, HBM],
        out_specs=VMEM,
        scratch_shapes=[stem_scratch, table_scratch, pltpu.SemaphoreType.DMA((spare + 1,))],
        compiler_params=LARGE,
        name="open_high",
    )(laid, hi_table)
    middle = pl.pallas_call(
        middle_kernel,
        out_shape=split_type,
        in_specs=[VMEM, HBM, HBM],
        out_specs=VMEM,
        scratch_shapes=[
            table_scratch,
            pltpu.VMEM((2, low, low), jnp.float32),
            pltpu.SemaphoreType.DMA((2,)),
        ],
        compiler_params=SMALL,
        name="middle_high_low",
    )(exchange(opened), hi_table, chain)
    closed = pl.pallas_call(
        close_kernel,
        out_shape=stem_type,
        in_specs=[VMEM, HBM],
        out_specs=HBM,
        scratch_shapes=[stem_scratch, table_scratch, pltpu.SemaphoreType.DMA((spare + 1,))],
        compiler_params=SMALL,
        name="close_high",
    )(exchange(middle), hi_table)
    return closed.reshape(-1, 2, LANES).transpose(1, 0, 2).reshape(stem.shape)


def body(stems, lo_table, hi_table, slice_bits):
    total = one_slice(stems[0], slice_bits[:1], lo_table, hi_table)
    for s in range(1, stems.shape[0]):
        total = total + one_slice(stems[s], slice_bits[s : s + 1], lo_table, hi_table)
    return total


def solution(mesh):
    placed = (P("groups", None, "stem"), P(), P(), P("groups", None))
    return jax.shard_map(
        body, mesh=mesh, in_specs=placed, out_specs=P(None, ("groups", "stem")), check_vma=False
    )
```

```python
import functools

import jax
import jax.numpy as jnp
from jax import lax
from jax.experimental import pallas as pl
from jax.experimental.pallas import tpu as pltpu
from jax.sharding import PartitionSpec as P

LANES = 128
SUBLANES = 8
VMEM = pl.BlockSpec(memory_space=pltpu.VMEM)
SMEM = pl.BlockSpec(memory_space=pltpu.SMEM)
HBM = pl.BlockSpec(memory_space=pltpu.HBM)
SMALL = pltpu.CompilerParams(vmem_limit_bytes=20 * 1024 * 1024)
LARGE = pltpu.CompilerParams(vmem_limit_bytes=56 * 1024 * 1024)


def halves(values):
    upper = values.astype(jnp.bfloat16)
    return upper, (values - upper.astype(jnp.float32)).astype(jnp.bfloat16)


def dot_halves(left, right):
    return jnp.dot(
        jnp.concatenate([left[0], left[0], left[1]], axis=1),
        jnp.concatenate([right[0], right[1], right[0]], axis=0),
        preferred_element_type=jnp.float32,
    )


def left_block(real_part, imag_part):
    upper = jnp.concatenate([real_part, -imag_part], axis=1)
    lower = jnp.concatenate([imag_part, real_part], axis=1)
    return jnp.concatenate([upper, lower], axis=0)


def left_halves(real_part, imag_part):
    return [left_block(*parts) for parts in zip(halves(real_part), halves(imag_part))]


def times_right(value, real_part, imag_part):
    high, low = value.shape[0] // 2, value.shape[1]
    sides = [jnp.concatenate(parts, axis=1) for parts in zip(halves(real_part), halves(imag_part))]
    value = dot_halves(halves(value), sides)
    return (
        value[:high, :low] - value[high:, low:],
        value[high:, :low] + value[:high, low:],
    )


def read_stem(stem_ref, high):
    tiles = stem_ref.shape[0] // (2 * high)
    parts = [
        jnp.concatenate(
            [stem_ref[pl.ds(2 * t + c, high, stride=2 * tiles), :] for t in range(tiles)], axis=1
        )
        for c in range(2)
    ]
    return jnp.concatenate(parts, axis=0)


def write_stem(stem_ref, value, high):
    tiles = stem_ref.shape[0] // (2 * high)
    for c in range(2):
        for t in range(tiles):
            stem_ref[pl.ds(2 * t + c, high, stride=2 * tiles), :] = value[
                c * high : (c + 1) * high, t * LANES : (t + 1) * LANES
            ]


def open_kernel(stem_ref, high_ref, out_ref, stem, table, sems):
    leading, spare, _, under, low = out_ref.shape
    high = leading * under
    table_copy = pltpu.make_async_copy(high_ref.at[0], table, sems.at[spare])
    table_copy.start()
    copies = [
        pltpu.make_async_copy(stem_ref.at[r], stem.at[r], sems.at[r]) for r in range(spare)
    ]
    for copy in copies:
        copy.start()
    table_copy.wait()
    matrix = left_halves(table[0], table[1])
    for r in range(spare):
        copies[r].wait()
        value = dot_halves(matrix, halves(read_stem(stem.at[r], high)))
        for c in range(2):
            out_ref[:, r, c] = value[c * high : (c + 1) * high].reshape(leading, under, low)


def chain_kernel(bits_ref, table_ref, out_ref, total):
    segments, _, _, low, _ = table_ref.shape

    def chosen(k):
        return table_ref.at[k, jnp.where(bits_ref[0, k] == 1, 1, 0)]

    def step(k, carry):
        table = chosen(k)
        total[...] = dot_halves(left_halves(table[0], table[1]), halves(total[...]))
        return carry

    for c in range(2):
        total[c * low : (c + 1) * low] = chosen(0)[c]
    lax.fori_loop(1, segments, step, 0)
    for c in range(2):
        out_ref[c] = total[c * low : (c + 1) * low].T


def middle_kernel(in_ref, high_ref, low_ref, out_ref, high_table, low_table, sems):
    leading, spare, _, under, low = in_ref.shape
    high = leading * under
    high_copy = pltpu.make_async_copy(high_ref.at[1], high_table, sems.at[0])
    low_copy = pltpu.make_async_copy(low_ref, low_table, sems.at[1])
    high_copy.start()
    low_copy.start()
    parts = [
        halves(jnp.concatenate([in_ref[:, r, c].reshape(high, low) for c in range(2)], axis=0))
        for r in range(spare)
    ]
    high_copy.wait()
    matrix = left_halves(high_table[0], high_table[1])
    parts = [dot_halves(matrix, part) for part in parts]
    low_copy.wait()
    for r in range(spare):
        for c, part in enumerate(times_right(parts[r], low_table[0], low_table[1])):
            out_ref[:, r, c] = part.reshape(leading, under, low)


def close_kernel(in_ref, high_ref, out_ref, held, table, sems):
    leading, spare, _, under, low = in_ref.shape
    high = leading * under
    table_copy = pltpu.make_async_copy(high_ref.at[2], table, sems.at[spare])
    table_copy.start()
    parts = [
        halves(jnp.concatenate([in_ref[:, r, c].reshape(high, low) for c in range(2)], axis=0))
        for r in range(spare)
    ]
    table_copy.wait()
    matrix = left_halves(table[0], table[1])
    copies = []
    for r in range(spare):
        write_stem(held.at[r], dot_halves(matrix, parts[r]), high)
        copies.append(pltpu.make_async_copy(held.at[r], out_ref.at[r], sems.at[r]))
        copies[-1].start()
    for copy in copies:
        copy.wait()


def layout_over(values, others):
    return tuple(tuple(value + other for other in others) for value in values)


def distances(layout):
    for n, array in enumerate(layout):
        for m, distance in enumerate(array):
            yield n, m, distance


def rows_by_distance(parts, me, under):
    devices = parts[0].shape[0] // under
    starts = [pl.multiple_of((me ^ d) * under, under) for d in range(devices)]
    return [
        jnp.concatenate([part[pl.ds(at, under), :] for at in starts], axis=0) for part in parts
    ]


def gather(in_refs, held, me, layout):
    under = in_refs[0].shape[2]
    for n, m, distance in distances(layout):
        at = pl.ds(pl.multiple_of((me ^ distance) * under, under), under)
        for c in range(2):
            held[c, at, :] = in_refs[n][m, c]
    return halves(jnp.concatenate([held[0], held[1]], axis=0))


def open_chunk(layout, me_ref, stem_ref, parts, out_refs):
    under = out_refs[0].shape[2]
    high = parts[0].shape[0]
    matrix = left_halves(*rows_by_distance(parts, me_ref[0], under))
    value = dot_halves(matrix, halves(read_stem(stem_ref, high)))
    for n, m, distance in distances(layout):
        for c in range(2):
            start = c * high + distance * under
            out_refs[n][m, c] = value[start : start + under]


def open_chunk_kernel(layout, me_ref, stem_ref, table, *out_refs):
    open_chunk(layout, me_ref, stem_ref, (table.at[0], table.at[1]), out_refs)


def open_first_kernel(layout, me_ref, packed_ref, *refs):
    *out_refs, table = refs
    _, high, _ = table.shape
    tiles = high // LANES
    rows = packed_ref.shape[0] - 2 * high * tiles
    matrix = packed_ref[rows:].reshape(2, high // SUBLANES, tiles, SUBLANES, LANES)
    for c in range(2):
        for t in range(tiles):
            part = matrix[c, :, t].reshape(high, LANES)
            table[c, :, t * LANES : (t + 1) * LANES] = part
    parts = table.at[0], table.at[1]
    open_chunk(layout, me_ref, packed_ref.at[pl.ds(0, rows)], parts, out_refs)


def turn_kernel(old, new, *refs):
    place = {distance: (n, m) for n, m, distance in distances(old)}
    for n, m, distance in distances(new):
        at = place[distance]
        refs[len(old) + n][m] = refs[at[0]][at[1]]


def middle_chunk_kernel(old, new, me_ref, table, low_table, *refs):
    *blocks, held, between = refs
    in_refs, out_refs = blocks[: len(old)], blocks[len(old) :]
    under = in_refs[0].shape[2]

    def stage(n, carry):
        @pl.when(n == 0)
        def high_modes():
            value = gather(in_refs, held, me_ref[0], old)
            matrix = left_halves(*rows_by_distance((table.at[0], table.at[1]), me_ref[0], under))
            between[...] = dot_halves(matrix, value)

        @pl.when(n == 1)
        def low_modes():
            parts = times_right(between[...], low_table[0], low_table[1])
            for n, m, distance in distances(new):
                for c in range(2):
                    out_refs[n][m, c] = parts[c][distance * under : (distance + 1) * under]

        return carry

    lax.fori_loop(0, 2, stage, 0)


def close_chunk(layout, me_ref, table, in_refs, held, stem):
    value = gather(in_refs, held, me_ref[0], layout)
    matrix = left_halves(table[0], table[1])
    write_stem(stem, dot_halves(matrix, value), table.shape[-1])


def close_first_kernel(layout, me_ref, table, *refs):
    *in_refs, out_ref, held = refs
    close_chunk(layout, me_ref, table, in_refs, held, out_ref)


def close_last_kernel(layout, me_ref, table, *refs):
    *in_refs, first_ref, out_ref, held, stem, sems = refs
    copies = [
        pltpu.make_async_copy(first_ref, out_ref.at[0], sems.at[0]),
        pltpu.make_async_copy(stem, out_ref.at[1], sems.at[1]),
    ]
    copies[0].start()
    close_chunk(layout, me_ref, table, in_refs, held, stem)
    copies[1].start()
    for copy in copies:
        copy.wait()


def chunks_by_permutes(laid, chain, hi_table, width):
    devices = lax.axis_size("stem")
    _, rows, _ = laid.shape
    high, low = hi_table.shape[-1], chain.shape[-1]
    under = high // devices
    me = lax.axis_index("stem").reshape(1)
    held = pltpu.VMEM((2, high, low), jnp.float32)
    upper = tuple(t * width for t in range(width))

    def lower(*first):
        return (0, *first, *(q for q in range(1, width) if q not in first))

    def tie(values, after):
        return lax.optimization_barrier((values, after))[0]

    def tied(values, at, after):
        return [tie(v, tuple(after)) if n == at else v for n, v in enumerate(values)]

    def blocks(layout):
        shapes = [(len(array), 2, under, low) for array in layout]
        return tuple(jax.ShapeDtypeStruct(shape, jnp.float32) for shape in shapes)

    def call(kernel, name, values, tables=(), out=None, scratch=()):
        specs = [SMEM] * bool(tables) + [VMEM] * (len(tables) + len(values))
        return pl.pallas_call(
            kernel,
            out_shape=blocks(out) if isinstance(out, tuple) else out,
            in_specs=specs,
            out_specs=(VMEM,) * len(out) if isinstance(out, tuple) else VMEM,
            scratch_shapes=list(scratch),
            compiler_params=SMALL,
            name=name,
        )(*[me] * bool(tables), *tables, *values)

    def send(values, layout):
        steps = [array[0] for array in layout]
        return [values[0]] + [
            lax.ppermute(value, "stem", [(i, i ^ step) for i in range(devices)])
            for value, step in zip(values[1:], steps[1:])
        ]

    def turn(old, new, values, name):
        return call(functools.partial(turn_kernel, old, new), name, values, out=new)

    def open_first(layout):
        tiles = high // LANES
        matrix = hi_table[0].reshape(2, high // SUBLANES, SUBLANES, tiles, LANES)
        matrix = matrix.transpose(0, 1, 3, 2, 4).reshape(-1, LANES)
        packed = jnp.concatenate([laid[0], matrix], axis=0)
        kernel = functools.partial(open_first_kernel, layout)
        scratch = [pltpu.VMEM((2, high, high), jnp.float32)]
        return call(kernel, "open_0", [], [packed], layout, scratch)

    def open_last(layout):
        kernel = functools.partial(open_chunk_kernel, layout)
        return call(kernel, "open_1", [], [stems[1], tables[0]], layout)

    def middle(old, new, values, name):
        kernel = functools.partial(middle_chunk_kernel, old, new)
        scratch = [held, pltpu.VMEM((2 * high, low), jnp.float32)]
        return call(kernel, name, values, [tables[1], chain], new, scratch)

    def close_first(layout, values):
        kernel = functools.partial(close_first_kernel, layout)
        out = jax.ShapeDtypeStruct(laid.shape[1:], jnp.float32)
        return call(kernel, "close_0", values, [tables[2]], out, [held])

    def close_last(layout, values, first):
        return pl.pallas_call(
            functools.partial(close_last_kernel, layout),
            out_shape=jax.ShapeDtypeStruct(laid.shape, jnp.float32),
            in_specs=[SMEM] + [VMEM] * (2 + len(layout)),
            out_specs=HBM,
            scratch_shapes=[
                held,
                pltpu.VMEM((rows, LANES), jnp.float32),
                pltpu.SemaphoreType.DMA((2,)),
            ],
            compiler_params=SMALL,
            name="close_1",
        )(me, tables[2], *values, first)

    orders = [lower(width // 2), lower(width // 2), lower(), lower(width // 2)]
    uppers = [layout_over(upper, order) for order in orders]
    lowers = [layout_over(order, upper) for order in orders]

    ahead = open_first(uppers[0])
    stems, tables = tie((laid, hi_table), ahead[0])
    behind = open_last(lowers[1])
    ahead = send(ahead, uppers[0])
    behind = send(behind, lowers[1])
    behind = turn(lowers[1], uppers[1], tied(behind, 0, [*ahead[1:3], chain]), "turn_1_in")
    behind = send(behind, uppers[1])
    ahead = turn(uppers[0], lowers[0], ahead, "turn_0_in")
    ahead = send(ahead, lowers[0])
    ahead = middle(lowers[0], uppers[2], tied(ahead, 0, behind[1:3]), "middle_0")
    ahead = send(ahead, uppers[2])
    behind = middle(uppers[1], lowers[3], behind, "middle_1")
    behind = send(behind, lowers[3])
    behind = turn(lowers[3], uppers[3], tied(behind, 2, ahead[1:3]), "turn_1_out")
    behind = send(behind, uppers[3])
    ahead = turn(uppers[2], lowers[2], ahead, "turn_0_out")
    ahead = send(ahead, lowers[2])
    first = close_first(lowers[2], tied(ahead, 0, behind[1:3]))
    return close_last(uppers[3], behind, first)


def one_slice(stem, bits, lo_table, hi_table):
    leading = lax.axis_size("stem")
    segments, _, high, _ = hi_table.shape
    low = lo_table.shape[-1]
    rows = high * 2 * (low // LANES)
    spare = stem.size // (rows * LANES)
    under = high // leading
    direct = under % SUBLANES == 0
    kept = (leading, under) if direct else (1, high)
    split_shape = (kept[0], spare, 2, kept[1], low)
    split_type = jax.ShapeDtypeStruct(split_shape, jnp.float32)
    stem_type = jax.ShapeDtypeStruct((spare, rows, LANES), jnp.float32)
    stem_scratch = pltpu.VMEM(stem_type.shape, jnp.float32)

    def exchange(values):
        if not direct:
            values = values.reshape(spare, 2, leading, under, low).transpose(2, 0, 1, 3, 4)
        values = lax.all_to_all(values, "stem", split_axis=0, concat_axis=0, tiled=True)
        if not direct:
            values = values.transpose(1, 2, 0, 3, 4).reshape(split_shape)
        return values

    laid = stem.reshape(2, stem.shape[1] // LANES, LANES).transpose(1, 0, 2)
    laid = laid.reshape(stem_type.shape)
    chain = pl.pallas_call(
        chain_kernel,
        out_shape=jax.ShapeDtypeStruct((2, low, low), jnp.float32),
        in_specs=[SMEM, VMEM],
        out_specs=VMEM,
        scratch_shapes=[pltpu.VMEM((2 * low, low), jnp.float32)],
        compiler_params=SMALL,
        name="low_chain",
    )(bits, lo_table)
    width = 1 << ((leading.bit_length() - 1) // 2)
    if direct and spare == 2 and width > 1 and width * width == leading:
        closed = chunks_by_permutes(laid, chain, hi_table, width)
        return closed.reshape(-1, 2, LANES).transpose(1, 0, 2).reshape(stem.shape)
    table_scratch = pltpu.VMEM((2, high, high), jnp.float32)
    opened = pl.pallas_call(
        open_kernel,
        out_shape=split_type,
        in_specs=[HBM, HBM],
        out_specs=VMEM,
        scratch_shapes=[stem_scratch, table_scratch, pltpu.SemaphoreType.DMA((spare + 1,))],
        compiler_params=LARGE,
        name="open_high",
    )(laid, hi_table)
    middle = pl.pallas_call(
        middle_kernel,
        out_shape=split_type,
        in_specs=[VMEM, HBM, HBM],
        out_specs=VMEM,
        scratch_shapes=[
            table_scratch,
            pltpu.VMEM((2, low, low), jnp.float32),
            pltpu.SemaphoreType.DMA((2,)),
        ],
        compiler_params=SMALL,
        name="middle_high_low",
    )(exchange(opened), hi_table, chain)
    closed = pl.pallas_call(
        close_kernel,
        out_shape=stem_type,
        in_specs=[VMEM, HBM],
        out_specs=HBM,
        scratch_shapes=[stem_scratch, table_scratch, pltpu.SemaphoreType.DMA((spare + 1,))],
        compiler_params=SMALL,
        name="close_high",
    )(exchange(middle), hi_table)
    return closed.reshape(-1, 2, LANES).transpose(1, 0, 2).reshape(stem.shape)


def body(stems, lo_table, hi_table, slice_bits):
    total = one_slice(stems[0], slice_bits[:1], lo_table, hi_table)
    for s in range(1, stems.shape[0]):
        total = total + one_slice(stems[s], slice_bits[s : s + 1], lo_table, hi_table)
    return total


def solution(mesh):
    placed = (P("groups", None, "stem"), P(), P(), P("groups", None))
    return jax.shard_map(
        body, mesh=mesh, in_specs=placed, out_specs=P(None, ("groups", "stem")), check_vma=False
    )
```

```python
import functools

import jax
import jax.numpy as jnp
from jax import lax
from jax.experimental import pallas as pl
from jax.experimental.pallas import tpu as pltpu
from jax.sharding import PartitionSpec as P

LANES = 128
SUBLANES = 8
VMEM = pl.BlockSpec(memory_space=pltpu.VMEM)
SMEM = pl.BlockSpec(memory_space=pltpu.SMEM)
HBM = pl.BlockSpec(memory_space=pltpu.HBM)
SMALL = pltpu.CompilerParams(vmem_limit_bytes=20 * 1024 * 1024)
LARGE = pltpu.CompilerParams(vmem_limit_bytes=56 * 1024 * 1024)


def halves(values):
    upper = values.astype(jnp.bfloat16)
    return upper, (values - upper.astype(jnp.float32)).astype(jnp.bfloat16)


def dot_halves(left, right):
    return jnp.dot(
        jnp.concatenate([left[0], left[0], left[1]], axis=1),
        jnp.concatenate([right[0], right[1], right[0]], axis=0),
        preferred_element_type=jnp.float32,
    )


def left_block(real_part, imag_part):
    upper = jnp.concatenate([real_part, -imag_part], axis=1)
    lower = jnp.concatenate([imag_part, real_part], axis=1)
    return jnp.concatenate([upper, lower], axis=0)


def left_halves(real_part, imag_part):
    return [left_block(*parts) for parts in zip(halves(real_part), halves(imag_part))]


def times_right(value, real_part, imag_part):
    high, low = value.shape[0] // 2, value.shape[1]
    sides = [jnp.concatenate(parts, axis=1) for parts in zip(halves(real_part), halves(imag_part))]
    value = dot_halves(halves(value), sides)
    return (
        value[:high, :low] - value[high:, low:],
        value[high:, :low] + value[:high, low:],
    )


def read_stem(stem_ref, high):
    tiles = stem_ref.shape[0] // (2 * high)
    parts = [
        jnp.concatenate(
            [stem_ref[pl.ds(2 * t + c, high, stride=2 * tiles), :] for t in range(tiles)], axis=1
        )
        for c in range(2)
    ]
    return jnp.concatenate(parts, axis=0)


def write_stem(stem_ref, value, high):
    tiles = stem_ref.shape[0] // (2 * high)
    for c in range(2):
        for t in range(tiles):
            stem_ref[pl.ds(2 * t + c, high, stride=2 * tiles), :] = value[
                c * high : (c + 1) * high, t * LANES : (t + 1) * LANES
            ]


def open_kernel(stem_ref, high_ref, out_ref, stem, table, sems):
    leading, spare, _, under, low = out_ref.shape
    high = leading * under
    table_copy = pltpu.make_async_copy(high_ref.at[0], table, sems.at[spare])
    table_copy.start()
    copies = [
        pltpu.make_async_copy(stem_ref.at[r], stem.at[r], sems.at[r]) for r in range(spare)
    ]
    for copy in copies:
        copy.start()
    table_copy.wait()
    matrix = left_halves(table[0], table[1])
    for r in range(spare):
        copies[r].wait()
        value = dot_halves(matrix, halves(read_stem(stem.at[r], high)))
        for c in range(2):
            out_ref[:, r, c] = value[c * high : (c + 1) * high].reshape(leading, under, low)


def chain_kernel(bits_ref, table_ref, out_ref, total):
    segments, _, _, low, _ = table_ref.shape

    def chosen(k):
        return table_ref.at[k, jnp.where(bits_ref[0, k] == 1, 1, 0)]

    def step(k, carry):
        table = chosen(k)
        total[...] = dot_halves(left_halves(table[0], table[1]), halves(total[...]))
        return carry

    for c in range(2):
        total[c * low : (c + 1) * low] = chosen(0)[c]
    lax.fori_loop(1, segments, step, 0)
    for c in range(2):
        out_ref[c] = total[c * low : (c + 1) * low].T


def middle_kernel(in_ref, high_ref, low_ref, out_ref, high_table, low_table, sems):
    leading, spare, _, under, low = in_ref.shape
    high = leading * under
    high_copy = pltpu.make_async_copy(high_ref.at[1], high_table, sems.at[0])
    low_copy = pltpu.make_async_copy(low_ref, low_table, sems.at[1])
    high_copy.start()
    low_copy.start()
    parts = [
        halves(jnp.concatenate([in_ref[:, r, c].reshape(high, low) for c in range(2)], axis=0))
        for r in range(spare)
    ]
    high_copy.wait()
    matrix = left_halves(high_table[0], high_table[1])
    parts = [dot_halves(matrix, part) for part in parts]
    low_copy.wait()
    for r in range(spare):
        for c, part in enumerate(times_right(parts[r], low_table[0], low_table[1])):
            out_ref[:, r, c] = part.reshape(leading, under, low)


def close_kernel(in_ref, high_ref, out_ref, held, table, sems):
    leading, spare, _, under, low = in_ref.shape
    high = leading * under
    table_copy = pltpu.make_async_copy(high_ref.at[2], table, sems.at[spare])
    table_copy.start()
    parts = [
        halves(jnp.concatenate([in_ref[:, r, c].reshape(high, low) for c in range(2)], axis=0))
        for r in range(spare)
    ]
    table_copy.wait()
    matrix = left_halves(table[0], table[1])
    copies = []
    for r in range(spare):
        write_stem(held.at[r], dot_halves(matrix, parts[r]), high)
        copies.append(pltpu.make_async_copy(held.at[r], out_ref.at[r], sems.at[r]))
        copies[-1].start()
    for copy in copies:
        copy.wait()


def layout_over(values, others):
    return tuple(tuple(value + other for other in others) for value in values)


def distances(layout):
    for n, array in enumerate(layout):
        for m, distance in enumerate(array):
            yield n, m, distance


def rows_by_distance(parts, me, under):
    devices = parts[0].shape[0] // under
    starts = [pl.multiple_of((me ^ d) * under, under) for d in range(devices)]
    return [
        jnp.concatenate([part[pl.ds(at, under), :] for at in starts], axis=0) for part in parts
    ]


def gather(in_refs, held, me, layout):
    under = in_refs[0].shape[2]
    for n, m, distance in distances(layout):
        at = pl.ds(pl.multiple_of((me ^ distance) * under, under), under)
        for c in range(2):
            held[c, at, :] = in_refs[n][m, c]
    return halves(jnp.concatenate([held[0], held[1]], axis=0))


def open_chunk(layout, me_ref, stem_ref, parts, out_refs):
    under = out_refs[0].shape[2]
    high = parts[0].shape[0]
    matrix = left_halves(*rows_by_distance(parts, me_ref[0], under))
    value = dot_halves(matrix, halves(read_stem(stem_ref, high)))
    for n, m, distance in distances(layout):
        for c in range(2):
            start = c * high + distance * under
            out_refs[n][m, c] = value[start : start + under]


def open_chunk_kernel(layout, me_ref, stem_ref, table, *out_refs):
    open_chunk(layout, me_ref, stem_ref, (table.at[0], table.at[1]), out_refs)


def open_first_kernel(layout, me_ref, packed_ref, *refs):
    *out_refs, table = refs
    _, high, _ = table.shape
    tiles = high // LANES
    rows = packed_ref.shape[0] - 2 * high * tiles
    matrix = packed_ref[rows:].reshape(2, high // SUBLANES, tiles, SUBLANES, LANES)
    for c in range(2):
        for t in range(tiles):
            part = matrix[c, :, t].reshape(high, LANES)
            table[c, :, t * LANES : (t + 1) * LANES] = part
    parts = table.at[0], table.at[1]
    open_chunk(layout, me_ref, packed_ref.at[pl.ds(0, rows)], parts, out_refs)


def turn_kernel(old, new, *refs):
    place = {distance: (n, m) for n, m, distance in distances(old)}
    for n, m, distance in distances(new):
        at = place[distance]
        refs[len(old) + n][m] = refs[at[0]][at[1]]


def middle_chunk_kernel(old, new, me_ref, table, low_table, *refs):
    *blocks, held, between = refs
    in_refs, out_refs = blocks[: len(old)], blocks[len(old) :]
    under = in_refs[0].shape[2]

    def stage(n, carry):
        @pl.when(n == 0)
        def high_modes():
            value = gather(in_refs, held, me_ref[0], old)
            matrix = left_halves(*rows_by_distance((table.at[0], table.at[1]), me_ref[0], under))
            between[...] = dot_halves(matrix, value)

        @pl.when(n == 1)
        def low_modes():
            parts = times_right(between[...], low_table[0], low_table[1])
            for n, m, distance in distances(new):
                for c in range(2):
                    out_refs[n][m, c] = parts[c][distance * under : (distance + 1) * under]

        return carry

    lax.fori_loop(0, 2, stage, 0)


def close_chunk(layout, me_ref, table, in_refs, held, stem):
    value = gather(in_refs, held, me_ref[0], layout)
    matrix = left_halves(table[0], table[1])
    write_stem(stem, dot_halves(matrix, value), table.shape[-1])


def close_first_kernel(layout, me_ref, table, *refs):
    *in_refs, out_ref, held = refs
    close_chunk(layout, me_ref, table, in_refs, held, out_ref)


def close_last_kernel(layout, me_ref, table, *refs):
    *in_refs, first_ref, out_ref, held, stem, sems = refs
    copies = [
        pltpu.make_async_copy(first_ref, out_ref.at[0], sems.at[0]),
        pltpu.make_async_copy(stem, out_ref.at[1], sems.at[1]),
    ]
    copies[0].start()
    close_chunk(layout, me_ref, table, in_refs, held, stem)
    copies[1].start()
    for copy in copies:
        copy.wait()


def chunks_by_permutes(laid, chain, hi_table, width):
    devices = lax.axis_size("stem")
    _, rows, _ = laid.shape
    high, low = hi_table.shape[-1], chain.shape[-1]
    under = high // devices
    me = lax.axis_index("stem").reshape(1)
    held = pltpu.VMEM((2, high, low), jnp.float32)
    upper = tuple(t * width for t in range(width))

    def lower(*first):
        return (0, *first, *(q for q in range(1, width) if q not in first))

    def tie(values, after):
        return lax.optimization_barrier((values, after))[0]

    def tied(values, at, after):
        return [tie(v, tuple(after)) if n == at else v for n, v in enumerate(values)]

    def blocks(layout):
        shapes = [(len(array), 2, under, low) for array in layout]
        return tuple(jax.ShapeDtypeStruct(shape, jnp.float32) for shape in shapes)

    def call(kernel, name, values, tables=(), out=None, scratch=()):
        specs = [SMEM] * bool(tables) + [VMEM] * (len(tables) + len(values))
        return pl.pallas_call(
            kernel,
            out_shape=blocks(out) if isinstance(out, tuple) else out,
            in_specs=specs,
            out_specs=(VMEM,) * len(out) if isinstance(out, tuple) else VMEM,
            scratch_shapes=list(scratch),
            compiler_params=SMALL,
            name=name,
        )(*[me] * bool(tables), *tables, *values)

    def send(values, layout):
        steps = [array[0] for array in layout]
        return [values[0]] + [
            lax.ppermute(value, "stem", [(i, i ^ step) for i in range(devices)])
            for value, step in zip(values[1:], steps[1:])
        ]

    def turn(old, new, values, name):
        return call(functools.partial(turn_kernel, old, new), name, values, out=new)

    def open_first(layout):
        tiles = high // LANES
        matrix = hi_table[0].reshape(2, high // SUBLANES, SUBLANES, tiles, LANES)
        matrix = matrix.transpose(0, 1, 3, 2, 4).reshape(-1, LANES)
        packed = jnp.concatenate([laid[0], matrix], axis=0)
        kernel = functools.partial(open_first_kernel, layout)
        scratch = [pltpu.VMEM((2, high, high), jnp.float32)]
        return call(kernel, "open_0", [], [packed], layout, scratch)

    def open_last(layout):
        kernel = functools.partial(open_chunk_kernel, layout)
        return call(kernel, "open_1", [], [stems[1], tables[0]], layout)

    def middle(old, new, values, name):
        kernel = functools.partial(middle_chunk_kernel, old, new)
        scratch = [held, pltpu.VMEM((2 * high, low), jnp.float32)]
        return call(kernel, name, values, [tables[1], chain], new, scratch)

    def close_first(layout, values):
        kernel = functools.partial(close_first_kernel, layout)
        out = jax.ShapeDtypeStruct(laid.shape[1:], jnp.float32)
        return call(kernel, "close_0", values, [tables[2]], out, [held])

    def close_last(layout, values, first):
        return pl.pallas_call(
            functools.partial(close_last_kernel, layout),
            out_shape=jax.ShapeDtypeStruct(laid.shape, jnp.float32),
            in_specs=[SMEM] + [VMEM] * (2 + len(layout)),
            out_specs=HBM,
            scratch_shapes=[
                held,
                pltpu.VMEM((rows, LANES), jnp.float32),
                pltpu.SemaphoreType.DMA((2,)),
            ],
            compiler_params=SMALL,
            name="close_1",
        )(me, tables[2], *values, first)

    orders = [lower(width // 2), lower(width // 2), lower(1, width - 1), lower(width // 2)]
    uppers = [layout_over(upper, order) for order in orders]
    lowers = [layout_over(order, upper) for order in orders]

    ahead = open_first(uppers[0])
    stems, tables = tie((laid, hi_table), ahead[0])
    behind = open_last(lowers[1])
    ahead = send(ahead, uppers[0])
    behind = send(behind, lowers[1])
    behind = turn(lowers[1], uppers[1], tied(behind, 0, [*ahead[1:3], chain]), "turn_1_in")
    behind = send(behind, uppers[1])
    ahead = turn(uppers[0], lowers[0], ahead, "turn_0_in")
    ahead = send(ahead, lowers[0])
    ahead = middle(lowers[0], uppers[2], tied(ahead, 1, behind[1:3]), "middle_0")
    ahead = send(ahead, uppers[2])
    behind = middle(uppers[1], lowers[3], behind, "middle_1")
    behind = send(behind, lowers[3])
    behind = turn(lowers[3], uppers[3], tied(behind, 1, ahead[1:3]), "turn_1_out")
    behind = send(behind, uppers[3])
    ahead = turn(uppers[2], lowers[2], ahead, "turn_0_out")
    ahead = send(ahead, lowers[2])
    first = close_first(lowers[2], tied(ahead, 0, behind[1:3]))
    return close_last(uppers[3], behind, first)


def one_slice(stem, bits, lo_table, hi_table):
    leading = lax.axis_size("stem")
    segments, _, high, _ = hi_table.shape
    low = lo_table.shape[-1]
    rows = high * 2 * (low // LANES)
    spare = stem.size // (rows * LANES)
    under = high // leading
    direct = under % SUBLANES == 0
    kept = (leading, under) if direct else (1, high)
    split_shape = (kept[0], spare, 2, kept[1], low)
    split_type = jax.ShapeDtypeStruct(split_shape, jnp.float32)
    stem_type = jax.ShapeDtypeStruct((spare, rows, LANES), jnp.float32)
    stem_scratch = pltpu.VMEM(stem_type.shape, jnp.float32)

    def exchange(values):
        if not direct:
            values = values.reshape(spare, 2, leading, under, low).transpose(2, 0, 1, 3, 4)
        values = lax.all_to_all(values, "stem", split_axis=0, concat_axis=0, tiled=True)
        if not direct:
            values = values.transpose(1, 2, 0, 3, 4).reshape(split_shape)
        return values

    laid = stem.reshape(2, stem.shape[1] // LANES, LANES).transpose(1, 0, 2)
    laid = laid.reshape(stem_type.shape)
    chain = pl.pallas_call(
        chain_kernel,
        out_shape=jax.ShapeDtypeStruct((2, low, low), jnp.float32),
        in_specs=[SMEM, VMEM],
        out_specs=VMEM,
        scratch_shapes=[pltpu.VMEM((2 * low, low), jnp.float32)],
        compiler_params=SMALL,
        name="low_chain",
    )(bits, lo_table)
    width = 1 << ((leading.bit_length() - 1) // 2)
    if direct and spare == 2 and width > 1 and width * width == leading:
        closed = chunks_by_permutes(laid, chain, hi_table, width)
        return closed.reshape(-1, 2, LANES).transpose(1, 0, 2).reshape(stem.shape)
    table_scratch = pltpu.VMEM((2, high, high), jnp.float32)
    opened = pl.pallas_call(
        open_kernel,
        out_shape=split_type,
        in_specs=[HBM, HBM],
        out_specs=VMEM,
        scratch_shapes=[stem_scratch, table_scratch, pltpu.SemaphoreType.DMA((spare + 1,))],
        compiler_params=LARGE,
        name="open_high",
    )(laid, hi_table)
    middle = pl.pallas_call(
        middle_kernel,
        out_shape=split_type,
        in_specs=[VMEM, HBM, HBM],
        out_specs=VMEM,
        scratch_shapes=[
            table_scratch,
            pltpu.VMEM((2, low, low), jnp.float32),
            pltpu.SemaphoreType.DMA((2,)),
        ],
        compiler_params=SMALL,
        name="middle_high_low",
    )(exchange(opened), hi_table, chain)
    closed = pl.pallas_call(
        close_kernel,
        out_shape=stem_type,
        in_specs=[VMEM, HBM],
        out_specs=HBM,
        scratch_shapes=[stem_scratch, table_scratch, pltpu.SemaphoreType.DMA((spare + 1,))],
        compiler_params=SMALL,
        name="close_high",
    )(exchange(middle), hi_table)
    return closed.reshape(-1, 2, LANES).transpose(1, 0, 2).reshape(stem.shape)


def body(stems, lo_table, hi_table, slice_bits):
    total = one_slice(stems[0], slice_bits[:1], lo_table, hi_table)
    for s in range(1, stems.shape[0]):
        total = total + one_slice(stems[s], slice_bits[s : s + 1], lo_table, hi_table)
    return total


def solution(mesh):
    placed = (P("groups", None, "stem"), P(), P(), P("groups", None))
    return jax.shard_map(
        body, mesh=mesh, in_specs=placed, out_specs=P(None, ("groups", "stem")), check_vma=False
    )
```

```python
import functools

import jax
import jax.numpy as jnp
from jax import lax
from jax.experimental import pallas as pl
from jax.experimental.pallas import tpu as pltpu
from jax.sharding import PartitionSpec as P

LANES = 128
SUBLANES = 8
VMEM = pl.BlockSpec(memory_space=pltpu.VMEM)
SMEM = pl.BlockSpec(memory_space=pltpu.SMEM)
HBM = pl.BlockSpec(memory_space=pltpu.HBM)
SMALL = pltpu.CompilerParams(vmem_limit_bytes=20 * 1024 * 1024)
LARGE = pltpu.CompilerParams(vmem_limit_bytes=56 * 1024 * 1024)


def halves(values):
    upper = values.astype(jnp.bfloat16)
    return upper, (values - upper.astype(jnp.float32)).astype(jnp.bfloat16)


def dot_halves(left, right):
    return jnp.dot(
        jnp.concatenate([left[0], left[0], left[1]], axis=1),
        jnp.concatenate([right[0], right[1], right[0]], axis=0),
        preferred_element_type=jnp.float32,
    )


def left_block(real_part, imag_part):
    upper = jnp.concatenate([real_part, -imag_part], axis=1)
    lower = jnp.concatenate([imag_part, real_part], axis=1)
    return jnp.concatenate([upper, lower], axis=0)


def left_halves(real_part, imag_part):
    return [left_block(*parts) for parts in zip(halves(real_part), halves(imag_part))]


def times_left(real_part, imag_part, value):
    high = value.shape[0] // 2
    upper, lower = value[:high], value[high:]
    by_real = dot_halves(halves(real_part), halves(upper))
    by_imag = dot_halves(halves(imag_part), halves(lower))
    by_sums = dot_halves(halves(real_part + imag_part), halves(upper + lower))
    return jnp.concatenate([by_real - by_imag, by_sums - by_real - by_imag], axis=0)


def times_right(value, real_part, imag_part):
    high, low = value.shape[0] // 2, value.shape[1]
    sides = [jnp.concatenate(parts, axis=1) for parts in zip(halves(real_part), halves(imag_part))]
    value = dot_halves(halves(value), sides)
    return (
        value[:high, :low] - value[high:, low:],
        value[high:, :low] + value[:high, low:],
    )


def read_stem(stem_ref, high):
    tiles = stem_ref.shape[0] // (2 * high)
    parts = [
        jnp.concatenate(
            [stem_ref[pl.ds(2 * t + c, high, stride=2 * tiles), :] for t in range(tiles)], axis=1
        )
        for c in range(2)
    ]
    return jnp.concatenate(parts, axis=0)


def write_stem(stem_ref, value, high):
    tiles = stem_ref.shape[0] // (2 * high)
    for c in range(2):
        for t in range(tiles):
            stem_ref[pl.ds(2 * t + c, high, stride=2 * tiles), :] = value[
                c * high : (c + 1) * high, t * LANES : (t + 1) * LANES
            ]


def open_kernel(stem_ref, high_ref, out_ref, stem, table, sems):
    leading, spare, _, under, low = out_ref.shape
    high = leading * under
    table_copy = pltpu.make_async_copy(high_ref.at[0], table, sems.at[spare])
    table_copy.start()
    copies = [
        pltpu.make_async_copy(stem_ref.at[r], stem.at[r], sems.at[r]) for r in range(spare)
    ]
    for copy in copies:
        copy.start()
    table_copy.wait()
    matrix = left_halves(table[0], table[1])
    for r in range(spare):
        copies[r].wait()
        value = dot_halves(matrix, halves(read_stem(stem.at[r], high)))
        for c in range(2):
            out_ref[:, r, c] = value[c * high : (c + 1) * high].reshape(leading, under, low)


def chain_kernel(bits_ref, table_ref, out_ref, total):
    segments, _, _, low, _ = table_ref.shape

    def chosen(k):
        return table_ref.at[k, jnp.where(bits_ref[0, k] == 1, 1, 0)]

    def step(k, carry):
        table = chosen(k)
        total[...] = times_left(table[0], table[1], total[...])
        return carry

    for c in range(2):
        total[c * low : (c + 1) * low] = chosen(0)[c]
    lax.fori_loop(1, segments, step, 0)
    for c in range(2):
        out_ref[c] = total[c * low : (c + 1) * low].T


def middle_kernel(in_ref, high_ref, low_ref, out_ref, high_table, low_table, sems):
    leading, spare, _, under, low = in_ref.shape
    high = leading * under
    high_copy = pltpu.make_async_copy(high_ref.at[1], high_table, sems.at[0])
    low_copy = pltpu.make_async_copy(low_ref, low_table, sems.at[1])
    high_copy.start()
    low_copy.start()
    parts = [
        halves(jnp.concatenate([in_ref[:, r, c].reshape(high, low) for c in range(2)], axis=0))
        for r in range(spare)
    ]
    high_copy.wait()
    matrix = left_halves(high_table[0], high_table[1])
    parts = [dot_halves(matrix, part) for part in parts]
    low_copy.wait()
    for r in range(spare):
        for c, part in enumerate(times_right(parts[r], low_table[0], low_table[1])):
            out_ref[:, r, c] = part.reshape(leading, under, low)


def close_kernel(in_ref, high_ref, out_ref, held, table, sems):
    leading, spare, _, under, low = in_ref.shape
    high = leading * under
    table_copy = pltpu.make_async_copy(high_ref.at[2], table, sems.at[spare])
    table_copy.start()
    parts = [
        halves(jnp.concatenate([in_ref[:, r, c].reshape(high, low) for c in range(2)], axis=0))
        for r in range(spare)
    ]
    table_copy.wait()
    matrix = left_halves(table[0], table[1])
    copies = []
    for r in range(spare):
        write_stem(held.at[r], dot_halves(matrix, parts[r]), high)
        copies.append(pltpu.make_async_copy(held.at[r], out_ref.at[r], sems.at[r]))
        copies[-1].start()
    for copy in copies:
        copy.wait()


def layout_over(values, others):
    return tuple(tuple(value + other for other in others) for value in values)


def distances(layout):
    for n, array in enumerate(layout):
        for m, distance in enumerate(array):
            yield n, m, distance


def rows_by_distance(parts, me, under):
    devices = parts[0].shape[0] // under
    starts = [pl.multiple_of((me ^ d) * under, under) for d in range(devices)]
    return [
        jnp.concatenate([part[pl.ds(at, under), :] for at in starts], axis=0) for part in parts
    ]


def gather(in_refs, held, me, layout):
    under = in_refs[0].shape[2]
    for n, m, distance in distances(layout):
        at = pl.ds(pl.multiple_of((me ^ distance) * under, under), under)
        for c in range(2):
            held[c, at, :] = in_refs[n][m, c]
    return jnp.concatenate([held[0], held[1]], axis=0)


def open_chunk(layout, me_ref, stem_ref, parts, out_refs):
    under = out_refs[0].shape[2]
    high = parts[0].shape[0]
    value = times_left(*rows_by_distance(parts, me_ref[0], under), read_stem(stem_ref, high))
    for n, m, distance in distances(layout):
        for c in range(2):
            start = c * high + distance * under
            out_refs[n][m, c] = value[start : start + under]


def open_chunk_kernel(layout, me_ref, stem_ref, table, *out_refs):
    open_chunk(layout, me_ref, stem_ref, (table.at[0], table.at[1]), out_refs)


def open_first_kernel(layout, me_ref, packed_ref, *refs):
    *out_refs, table = refs
    _, high, _ = table.shape
    tiles = high // LANES
    rows = packed_ref.shape[0] - 2 * high * tiles
    matrix = packed_ref[rows:].reshape(2, high // SUBLANES, tiles, SUBLANES, LANES)
    for c in range(2):
        for t in range(tiles):
            part = matrix[c, :, t].reshape(high, LANES)
            table[c, :, t * LANES : (t + 1) * LANES] = part
    parts = table.at[0], table.at[1]
    open_chunk(layout, me_ref, packed_ref.at[pl.ds(0, rows)], parts, out_refs)


def turn_kernel(old, new, *refs):
    place = {distance: (n, m) for n, m, distance in distances(old)}
    for n, m, distance in distances(new):
        at = place[distance]
        refs[len(old) + n][m] = refs[at[0]][at[1]]


def middle_chunk_kernel(old, new, me_ref, table, low_table, *refs):
    *blocks, held, between = refs
    in_refs, out_refs = blocks[: len(old)], blocks[len(old) :]
    under = in_refs[0].shape[2]

    def stage(n, carry):
        @pl.when(n == 0)
        def high_modes():
            value = gather(in_refs, held, me_ref[0], old)
            parts = rows_by_distance((table.at[0], table.at[1]), me_ref[0], under)
            between[...] = times_left(*parts, value)

        @pl.when(n == 1)
        def low_modes():
            parts = times_right(between[...], low_table[0], low_table[1])
            for n, m, distance in distances(new):
                for c in range(2):
                    out_refs[n][m, c] = parts[c][distance * under : (distance + 1) * under]

        return carry

    lax.fori_loop(0, 2, stage, 0)


def close_chunk(layout, me_ref, table, in_refs, held, stem):
    value = gather(in_refs, held, me_ref[0], layout)
    write_stem(stem, times_left(table[0], table[1], value), table.shape[-1])


def close_first_kernel(layout, me_ref, table, *refs):
    *in_refs, out_ref, held = refs
    close_chunk(layout, me_ref, table, in_refs, held, out_ref)


def close_last_kernel(layout, me_ref, table, *refs):
    *in_refs, first_ref, out_ref, held, stem, sems = refs
    copies = [
        pltpu.make_async_copy(first_ref, out_ref.at[0], sems.at[0]),
        pltpu.make_async_copy(stem, out_ref.at[1], sems.at[1]),
    ]
    copies[0].start()
    close_chunk(layout, me_ref, table, in_refs, held, stem)
    copies[1].start()
    for copy in copies:
        copy.wait()


def chunks_by_permutes(laid, chain, hi_table, width):
    devices = lax.axis_size("stem")
    _, rows, _ = laid.shape
    high, low = hi_table.shape[-1], chain.shape[-1]
    under = high // devices
    me = lax.axis_index("stem").reshape(1)
    held = pltpu.VMEM((2, high, low), jnp.float32)
    upper = tuple(t * width for t in range(width))

    def lower(*first):
        return (0, *first, *(q for q in range(1, width) if q not in first))

    def tie(values, after):
        return lax.optimization_barrier((values, after))[0]

    def tied(values, at, after):
        return [tie(v, tuple(after)) if n == at else v for n, v in enumerate(values)]

    def blocks(layout):
        shapes = [(len(array), 2, under, low) for array in layout]
        return tuple(jax.ShapeDtypeStruct(shape, jnp.float32) for shape in shapes)

    def call(kernel, name, values, tables=(), out=None, scratch=()):
        specs = [SMEM] * bool(tables) + [VMEM] * (len(tables) + len(values))
        return pl.pallas_call(
            kernel,
            out_shape=blocks(out) if isinstance(out, tuple) else out,
            in_specs=specs,
            out_specs=(VMEM,) * len(out) if isinstance(out, tuple) else VMEM,
            scratch_shapes=list(scratch),
            compiler_params=SMALL,
            name=name,
        )(*[me] * bool(tables), *tables, *values)

    def send(values, layout):
        steps = [array[0] for array in layout]
        return [values[0]] + [
            lax.ppermute(value, "stem", [(i, i ^ step) for i in range(devices)])
            for value, step in zip(values[1:], steps[1:])
        ]

    def turn(old, new, values, name):
        return call(functools.partial(turn_kernel, old, new), name, values, out=new)

    def open_first(layout):
        tiles = high // LANES
        matrix = hi_table[0].reshape(2, high // SUBLANES, SUBLANES, tiles, LANES)
        matrix = matrix.transpose(0, 1, 3, 2, 4).reshape(-1, LANES)
        packed = jnp.concatenate([laid[0], matrix], axis=0)
        kernel = functools.partial(open_first_kernel, layout)
        scratch = [pltpu.VMEM((2, high, high), jnp.float32)]
        return call(kernel, "open_0", [], [packed], layout, scratch)

    def open_last(layout):
        kernel = functools.partial(open_chunk_kernel, layout)
        return call(kernel, "open_1", [], [stems[1], tables[0]], layout)

    def middle(old, new, values, name):
        kernel = functools.partial(middle_chunk_kernel, old, new)
        scratch = [held, pltpu.VMEM((2 * high, low), jnp.float32)]
        return call(kernel, name, values, [tables[1], chain], new, scratch)

    def close_first(layout, values):
        kernel = functools.partial(close_first_kernel, layout)
        out = jax.ShapeDtypeStruct(laid.shape[1:], jnp.float32)
        return call(kernel, "close_0", values, [tables[2]], out, [held])

    def close_last(layout, values, first):
        return pl.pallas_call(
            functools.partial(close_last_kernel, layout),
            out_shape=jax.ShapeDtypeStruct(laid.shape, jnp.float32),
            in_specs=[SMEM] + [VMEM] * (2 + len(layout)),
            out_specs=HBM,
            scratch_shapes=[
                held,
                pltpu.VMEM((rows, LANES), jnp.float32),
                pltpu.SemaphoreType.DMA((2,)),
            ],
            compiler_params=SMALL,
            name="close_1",
        )(me, tables[2], *values, first)

    orders = [lower(width // 2), lower(width // 2), lower(1, width - 1), lower(width // 2)]
    uppers = [layout_over(upper, order) for order in orders]
    lowers = [layout_over(order, upper) for order in orders]

    ahead = open_first(uppers[0])
    stems, tables = tie((laid, hi_table), ahead[0])
    behind = open_last(lowers[1])
    ahead = send(ahead, uppers[0])
    behind = send(behind, lowers[1])
    behind = turn(lowers[1], uppers[1], tied(behind, 0, [*ahead[1:3], chain]), "turn_1_in")
    behind = send(behind, uppers[1])
    ahead = turn(uppers[0], lowers[0], ahead, "turn_0_in")
    ahead = send(ahead, lowers[0])
    ahead = middle(lowers[0], uppers[2], tied(ahead, 1, behind[1:3]), "middle_0")
    ahead = send(ahead, uppers[2])
    behind = middle(uppers[1], lowers[3], behind, "middle_1")
    behind = send(behind, lowers[3])
    behind = turn(lowers[3], uppers[3], tied(behind, 1, ahead[1:3]), "turn_1_out")
    behind = send(behind, uppers[3])
    ahead = turn(uppers[2], lowers[2], ahead, "turn_0_out")
    ahead = send(ahead, lowers[2])
    first = close_first(lowers[2], tied(ahead, 0, behind[1:3]))
    return close_last(uppers[3], behind, first)


def one_slice(stem, bits, lo_table, hi_table):
    leading = lax.axis_size("stem")
    segments, _, high, _ = hi_table.shape
    low = lo_table.shape[-1]
    rows = high * 2 * (low // LANES)
    spare = stem.size // (rows * LANES)
    under = high // leading
    direct = under % SUBLANES == 0
    kept = (leading, under) if direct else (1, high)
    split_shape = (kept[0], spare, 2, kept[1], low)
    split_type = jax.ShapeDtypeStruct(split_shape, jnp.float32)
    stem_type = jax.ShapeDtypeStruct((spare, rows, LANES), jnp.float32)
    stem_scratch = pltpu.VMEM(stem_type.shape, jnp.float32)

    def exchange(values):
        if not direct:
            values = values.reshape(spare, 2, leading, under, low).transpose(2, 0, 1, 3, 4)
        values = lax.all_to_all(values, "stem", split_axis=0, concat_axis=0, tiled=True)
        if not direct:
            values = values.transpose(1, 2, 0, 3, 4).reshape(split_shape)
        return values

    laid = stem.reshape(2, stem.shape[1] // LANES, LANES).transpose(1, 0, 2)
    laid = laid.reshape(stem_type.shape)
    chain = pl.pallas_call(
        chain_kernel,
        out_shape=jax.ShapeDtypeStruct((2, low, low), jnp.float32),
        in_specs=[SMEM, VMEM],
        out_specs=VMEM,
        scratch_shapes=[pltpu.VMEM((2 * low, low), jnp.float32)],
        compiler_params=SMALL,
        name="low_chain",
    )(bits, lo_table)
    width = 1 << ((leading.bit_length() - 1) // 2)
    if direct and spare == 2 and width > 1 and width * width == leading:
        closed = chunks_by_permutes(laid, chain, hi_table, width)
        return closed.reshape(-1, 2, LANES).transpose(1, 0, 2).reshape(stem.shape)
    table_scratch = pltpu.VMEM((2, high, high), jnp.float32)
    opened = pl.pallas_call(
        open_kernel,
        out_shape=split_type,
        in_specs=[HBM, HBM],
        out_specs=VMEM,
        scratch_shapes=[stem_scratch, table_scratch, pltpu.SemaphoreType.DMA((spare + 1,))],
        compiler_params=LARGE,
        name="open_high",
    )(laid, hi_table)
    middle = pl.pallas_call(
        middle_kernel,
        out_shape=split_type,
        in_specs=[VMEM, HBM, HBM],
        out_specs=VMEM,
        scratch_shapes=[
            table_scratch,
            pltpu.VMEM((2, low, low), jnp.float32),
            pltpu.SemaphoreType.DMA((2,)),
        ],
        compiler_params=SMALL,
        name="middle_high_low",
    )(exchange(opened), hi_table, chain)
    closed = pl.pallas_call(
        close_kernel,
        out_shape=stem_type,
        in_specs=[VMEM, HBM],
        out_specs=HBM,
        scratch_shapes=[stem_scratch, table_scratch, pltpu.SemaphoreType.DMA((spare + 1,))],
        compiler_params=SMALL,
        name="close_high",
    )(exchange(middle), hi_table)
    return closed.reshape(-1, 2, LANES).transpose(1, 0, 2).reshape(stem.shape)


def body(stems, lo_table, hi_table, slice_bits):
    total = one_slice(stems[0], slice_bits[:1], lo_table, hi_table)
    for s in range(1, stems.shape[0]):
        total = total + one_slice(stems[s], slice_bits[s : s + 1], lo_table, hi_table)
    return total


def solution(mesh):
    placed = (P("groups", None, "stem"), P(), P(), P("groups", None))
    return jax.shard_map(
        body, mesh=mesh, in_specs=placed, out_specs=P(None, ("groups", "stem")), check_vma=False
    )
```

```python
import functools

import jax
import jax.numpy as jnp
from jax import lax
from jax.experimental import pallas as pl
from jax.experimental.pallas import tpu as pltpu
from jax.sharding import PartitionSpec as P

LANES = 128
SUBLANES = 8
VMEM = pl.BlockSpec(memory_space=pltpu.VMEM)
SMEM = pl.BlockSpec(memory_space=pltpu.SMEM)
HBM = pl.BlockSpec(memory_space=pltpu.HBM)
SMALL = pltpu.CompilerParams(vmem_limit_bytes=20 * 1024 * 1024)
LARGE = pltpu.CompilerParams(vmem_limit_bytes=56 * 1024 * 1024)


def halves(values):
    upper = values.astype(jnp.bfloat16)
    return upper, (values - upper.astype(jnp.float32)).astype(jnp.bfloat16)


def dot_halves(left, right):
    return jnp.dot(
        jnp.concatenate([left[0], left[0], left[1]], axis=1),
        jnp.concatenate([right[0], right[1], right[0]], axis=0),
        preferred_element_type=jnp.float32,
    )


def left_block(real_part, imag_part):
    upper = jnp.concatenate([real_part, -imag_part], axis=1)
    lower = jnp.concatenate([imag_part, real_part], axis=1)
    return jnp.concatenate([upper, lower], axis=0)


def left_halves(real_part, imag_part):
    return [left_block(*parts) for parts in zip(halves(real_part), halves(imag_part))]


def times_left(real_part, imag_part, value):
    high = value.shape[0] // 2
    upper, lower = value[:high], value[high:]
    by_real = dot_halves(halves(real_part), halves(upper))
    by_imag = dot_halves(halves(imag_part), halves(lower))
    by_sums = dot_halves(halves(real_part + imag_part), halves(upper + lower))
    return jnp.concatenate([by_real - by_imag, by_sums - by_real - by_imag], axis=0)


def times_right(value, real_part, imag_part):
    high, low = value.shape[0] // 2, value.shape[1]
    sides = [jnp.concatenate(parts, axis=1) for parts in zip(halves(real_part), halves(imag_part))]
    value = dot_halves(halves(value), sides)
    return (
        value[:high, :low] - value[high:, low:],
        value[high:, :low] + value[:high, low:],
    )


def read_stem(stem_ref, high):
    tiles = stem_ref.shape[0] // (2 * high)
    parts = [
        jnp.concatenate(
            [stem_ref[pl.ds(2 * t + c, high, stride=2 * tiles), :] for t in range(tiles)], axis=1
        )
        for c in range(2)
    ]
    return jnp.concatenate(parts, axis=0)


def write_stem(stem_ref, value, high):
    tiles = stem_ref.shape[0] // (2 * high)
    for c in range(2):
        for t in range(tiles):
            stem_ref[pl.ds(2 * t + c, high, stride=2 * tiles), :] = value[
                c * high : (c + 1) * high, t * LANES : (t + 1) * LANES
            ]


def open_kernel(stem_ref, high_ref, out_ref, stem, table, sems):
    leading, spare, _, under, low = out_ref.shape
    high = leading * under
    table_copy = pltpu.make_async_copy(high_ref.at[0], table, sems.at[spare])
    table_copy.start()
    copies = [
        pltpu.make_async_copy(stem_ref.at[r], stem.at[r], sems.at[r]) for r in range(spare)
    ]
    for copy in copies:
        copy.start()
    table_copy.wait()
    matrix = left_halves(table[0], table[1])
    for r in range(spare):
        copies[r].wait()
        value = dot_halves(matrix, halves(read_stem(stem.at[r], high)))
        for c in range(2):
            out_ref[:, r, c] = value[c * high : (c + 1) * high].reshape(leading, under, low)


def chain_kernel(bits_ref, table_ref, out_ref, total):
    segments, _, _, low, _ = table_ref.shape

    def chosen(k):
        return table_ref.at[k, jnp.where(bits_ref[0, k] == 1, 1, 0)]

    def step(k, carry):
        table = chosen(k)
        total[...] = times_left(table[0], table[1], total[...])
        return carry

    for c in range(2):
        total[c * low : (c + 1) * low] = chosen(0)[c]
    lax.fori_loop(1, segments, step, 0)
    for c in range(2):
        out_ref[c] = total[c * low : (c + 1) * low].T


def middle_kernel(in_ref, high_ref, low_ref, out_ref, high_table, low_table, sems):
    leading, spare, _, under, low = in_ref.shape
    high = leading * under
    high_copy = pltpu.make_async_copy(high_ref.at[1], high_table, sems.at[0])
    low_copy = pltpu.make_async_copy(low_ref, low_table, sems.at[1])
    high_copy.start()
    low_copy.start()
    parts = [
        halves(jnp.concatenate([in_ref[:, r, c].reshape(high, low) for c in range(2)], axis=0))
        for r in range(spare)
    ]
    high_copy.wait()
    matrix = left_halves(high_table[0], high_table[1])
    parts = [dot_halves(matrix, part) for part in parts]
    low_copy.wait()
    for r in range(spare):
        for c, part in enumerate(times_right(parts[r], low_table[0], low_table[1])):
            out_ref[:, r, c] = part.reshape(leading, under, low)


def close_kernel(in_ref, high_ref, out_ref, held, table, sems):
    leading, spare, _, under, low = in_ref.shape
    high = leading * under
    table_copy = pltpu.make_async_copy(high_ref.at[2], table, sems.at[spare])
    table_copy.start()
    parts = [
        halves(jnp.concatenate([in_ref[:, r, c].reshape(high, low) for c in range(2)], axis=0))
        for r in range(spare)
    ]
    table_copy.wait()
    matrix = left_halves(table[0], table[1])
    copies = []
    for r in range(spare):
        write_stem(held.at[r], dot_halves(matrix, parts[r]), high)
        copies.append(pltpu.make_async_copy(held.at[r], out_ref.at[r], sems.at[r]))
        copies[-1].start()
    for copy in copies:
        copy.wait()


def layout_over(values, others):
    return tuple(tuple(value + other for other in others) for value in values)


def distances(layout):
    for n, array in enumerate(layout):
        for m, distance in enumerate(array):
            yield n, m, distance


def rows_by_distance(parts, me, under):
    devices = parts[0].shape[0] // under
    starts = [pl.multiple_of((me ^ d) * under, under) for d in range(devices)]
    return [
        jnp.concatenate([part[pl.ds(at, under), :] for at in starts], axis=0) for part in parts
    ]


def gather(in_refs, held, me, layout):
    under = in_refs[0].shape[2]
    for n, m, distance in distances(layout):
        at = pl.ds(pl.multiple_of((me ^ distance) * under, under), under)
        for c in range(2):
            held[c, at, :] = in_refs[n][m, c]
    return jnp.concatenate([held[0], held[1]], axis=0)


def open_chunk(layout, me_ref, stem_ref, parts, out_refs):
    under = out_refs[0].shape[2]
    high = parts[0].shape[0]
    value = times_left(*rows_by_distance(parts, me_ref[0], under), read_stem(stem_ref, high))
    for n, m, distance in distances(layout):
        for c in range(2):
            start = c * high + distance * under
            out_refs[n][m, c] = value[start : start + under]


def open_chunk_kernel(layout, me_ref, stem_ref, table, *out_refs):
    open_chunk(layout, me_ref, stem_ref, (table.at[0], table.at[1]), out_refs)


def open_first_kernel(layout, me_ref, packed_ref, *refs):
    *out_refs, table = refs
    _, high, _ = table.shape
    tiles = high // LANES
    rows = packed_ref.shape[0] - 2 * high * tiles
    matrix = packed_ref[rows:].reshape(2, high // SUBLANES, tiles, SUBLANES, LANES)
    for c in range(2):
        for t in range(tiles):
            part = matrix[c, :, t].reshape(high, LANES)
            table[c, :, t * LANES : (t + 1) * LANES] = part
    parts = table.at[0], table.at[1]
    open_chunk(layout, me_ref, packed_ref.at[pl.ds(0, rows)], parts, out_refs)


def turn_kernel(old, new, *refs):
    place = {distance: (n, m) for n, m, distance in distances(old)}
    for n, m, distance in distances(new):
        at = place[distance]
        refs[len(old) + n][m] = refs[at[0]][at[1]]


def middle_chunk_kernel(old, new, me_ref, table, low_table, *refs):
    *blocks, held, between = refs
    in_refs, out_refs = blocks[: len(old)], blocks[len(old) :]
    under = in_refs[0].shape[2]

    def stage(n, carry):
        @pl.when(n == 0)
        def high_modes():
            value = gather(in_refs, held, me_ref[0], old)
            parts = rows_by_distance((table.at[0], table.at[1]), me_ref[0], under)
            between[...] = times_left(*parts, value)

        @pl.when(n == 1)
        def low_modes():
            parts = times_right(between[...], low_table[0], low_table[1])
            for n, m, distance in distances(new):
                for c in range(2):
                    out_refs[n][m, c] = parts[c][distance * under : (distance + 1) * under]

        return carry

    lax.fori_loop(0, 2, stage, 0)


def close_chunk(layout, me_ref, table, in_refs, held, stem):
    value = gather(in_refs, held, me_ref[0], layout)
    write_stem(stem, times_left(table[0], table[1], value), table.shape[-1])


def close_first_kernel(layout, me_ref, table, *refs):
    *in_refs, out_ref, held = refs
    close_chunk(layout, me_ref, table, in_refs, held, out_ref)


def close_last_kernel(layout, me_ref, table, *refs):
    *in_refs, first_ref, out_ref, held, stem, sems = refs
    copies = [
        pltpu.make_async_copy(first_ref, out_ref.at[0], sems.at[0]),
        pltpu.make_async_copy(stem, out_ref.at[1], sems.at[1]),
    ]
    copies[0].start()
    close_chunk(layout, me_ref, table, in_refs, held, stem)
    copies[1].start()
    for copy in copies:
        copy.wait()


def chunks_by_permutes(laid, chain, hi_table, width):
    devices = lax.axis_size("stem")
    _, rows, _ = laid.shape
    high, low = hi_table.shape[-1], chain.shape[-1]
    under = high // devices
    me = lax.axis_index("stem").reshape(1)
    held = pltpu.VMEM((2, high, low), jnp.float32)
    upper = tuple(t * width for t in range(width))

    def lower(*first):
        return (0, *first, *(q for q in range(1, width) if q not in first))

    def tie(values, after):
        return lax.optimization_barrier((values, after))[0]

    def tied(values, at, after):
        return [tie(v, tuple(after)) if n == at else v for n, v in enumerate(values)]

    def blocks(layout):
        shapes = [(len(array), 2, under, low) for array in layout]
        return tuple(jax.ShapeDtypeStruct(shape, jnp.float32) for shape in shapes)

    def call(kernel, name, values, tables=(), out=None, scratch=()):
        specs = [SMEM] * bool(tables) + [VMEM] * (len(tables) + len(values))
        return pl.pallas_call(
            kernel,
            out_shape=blocks(out) if isinstance(out, tuple) else out,
            in_specs=specs,
            out_specs=(VMEM,) * len(out) if isinstance(out, tuple) else VMEM,
            scratch_shapes=list(scratch),
            compiler_params=SMALL,
            name=name,
        )(*[me] * bool(tables), *tables, *values)

    def send(values, layout):
        steps = [array[0] for array in layout]
        return [values[0]] + [
            lax.ppermute(value, "stem", [(i, i ^ step) for i in range(devices)])
            for value, step in zip(values[1:], steps[1:])
        ]

    def turn(old, new, values, name):
        return call(functools.partial(turn_kernel, old, new), name, values, out=new)

    def open_first(layout):
        tiles = high // LANES
        matrix = hi_table[0].reshape(2, high // SUBLANES, SUBLANES, tiles, LANES)
        matrix = matrix.transpose(0, 1, 3, 2, 4).reshape(-1, LANES)
        packed = jnp.concatenate([laid[0], matrix], axis=0)
        kernel = functools.partial(open_first_kernel, layout)
        scratch = [pltpu.VMEM((2, high, high), jnp.float32)]
        return call(kernel, "open_0", [], [packed], layout, scratch)

    def open_last(layout):
        kernel = functools.partial(open_chunk_kernel, layout)
        return call(kernel, "open_1", [], [stems[1], tables[0]], layout)

    def middle(old, new, values, name):
        kernel = functools.partial(middle_chunk_kernel, old, new)
        scratch = [held, pltpu.VMEM((2 * high, low), jnp.float32)]
        return call(kernel, name, values, [tables[1], chain], new, scratch)

    def close_first(layout, values):
        kernel = functools.partial(close_first_kernel, layout)
        out = jax.ShapeDtypeStruct(laid.shape[1:], jnp.float32)
        return call(kernel, "close_0", values, [tables[2]], out, [held])

    def close_last(layout, values, first):
        return pl.pallas_call(
            functools.partial(close_last_kernel, layout),
            out_shape=jax.ShapeDtypeStruct(laid.shape, jnp.float32),
            in_specs=[SMEM] + [VMEM] * (2 + len(layout)),
            out_specs=HBM,
            scratch_shapes=[
                held,
                pltpu.VMEM((rows, LANES), jnp.float32),
                pltpu.SemaphoreType.DMA((2,)),
            ],
            compiler_params=SMALL,
            name="close_1",
        )(me, tables[2], *values, first)

    orders = [lower(width // 2), lower(width // 2), lower(1, width - 1), lower(width // 2)]
    uppers = [layout_over(upper, order) for order in orders]
    lowers = [layout_over(order, upper) for order in orders]

    ahead = open_first(uppers[0])
    stems, tables = tie((laid, hi_table), ahead[0])
    behind = open_last(lowers[1])
    ahead = send(ahead, uppers[0])
    behind = send(behind, lowers[1])
    behind = turn(lowers[1], uppers[1], tied(behind, 0, [chain, *ahead[1:3]]), "turn_1_in")
    behind = send(behind, uppers[1])
    ahead = turn(uppers[0], lowers[0], ahead, "turn_0_in")
    ahead = send(ahead, lowers[0])
    ahead = middle(lowers[0], uppers[2], tied(ahead, 1, behind[1:3]), "middle_0")
    ahead = send(ahead, uppers[2])
    behind = middle(uppers[1], lowers[3], behind, "middle_1")
    behind = send(behind, lowers[3])
    behind = turn(lowers[3], uppers[3], tied(behind, 1, ahead[1:3]), "turn_1_out")
    behind = send(behind, uppers[3])
    ahead = turn(uppers[2], lowers[2], ahead, "turn_0_out")
    ahead = send(ahead, lowers[2])
    first = close_first(lowers[2], tied(ahead, 0, behind[1:3]))
    return close_last(uppers[3], behind, first)


def one_slice(stem, bits, lo_table, hi_table):
    leading = lax.axis_size("stem")
    segments, _, high, _ = hi_table.shape
    low = lo_table.shape[-1]
    rows = high * 2 * (low // LANES)
    spare = stem.size // (rows * LANES)
    under = high // leading
    direct = under % SUBLANES == 0
    kept = (leading, under) if direct else (1, high)
    split_shape = (kept[0], spare, 2, kept[1], low)
    split_type = jax.ShapeDtypeStruct(split_shape, jnp.float32)
    stem_type = jax.ShapeDtypeStruct((spare, rows, LANES), jnp.float32)
    stem_scratch = pltpu.VMEM(stem_type.shape, jnp.float32)

    def exchange(values):
        if not direct:
            values = values.reshape(spare, 2, leading, under, low).transpose(2, 0, 1, 3, 4)
        values = lax.all_to_all(values, "stem", split_axis=0, concat_axis=0, tiled=True)
        if not direct:
            values = values.transpose(1, 2, 0, 3, 4).reshape(split_shape)
        return values

    laid = stem.reshape(2, stem.shape[1] // LANES, LANES).transpose(1, 0, 2)
    laid = laid.reshape(stem_type.shape)
    chain = pl.pallas_call(
        chain_kernel,
        out_shape=jax.ShapeDtypeStruct((2, low, low), jnp.float32),
        in_specs=[SMEM, VMEM],
        out_specs=VMEM,
        scratch_shapes=[pltpu.VMEM((2 * low, low), jnp.float32)],
        compiler_params=SMALL,
        name="low_chain",
    )(bits, lo_table)
    width = 1 << ((leading.bit_length() - 1) // 2)
    if direct and spare == 2 and width > 1 and width * width == leading:
        closed = chunks_by_permutes(laid, chain, hi_table, width)
        return closed.reshape(-1, 2, LANES).transpose(1, 0, 2).reshape(stem.shape)
    table_scratch = pltpu.VMEM((2, high, high), jnp.float32)
    opened = pl.pallas_call(
        open_kernel,
        out_shape=split_type,
        in_specs=[HBM, HBM],
        out_specs=VMEM,
        scratch_shapes=[stem_scratch, table_scratch, pltpu.SemaphoreType.DMA((spare + 1,))],
        compiler_params=LARGE,
        name="open_high",
    )(laid, hi_table)
    middle = pl.pallas_call(
        middle_kernel,
        out_shape=split_type,
        in_specs=[VMEM, HBM, HBM],
        out_specs=VMEM,
        scratch_shapes=[
            table_scratch,
            pltpu.VMEM((2, low, low), jnp.float32),
            pltpu.SemaphoreType.DMA((2,)),
        ],
        compiler_params=SMALL,
        name="middle_high_low",
    )(exchange(opened), hi_table, chain)
    closed = pl.pallas_call(
        close_kernel,
        out_shape=stem_type,
        in_specs=[VMEM, HBM],
        out_specs=HBM,
        scratch_shapes=[stem_scratch, table_scratch, pltpu.SemaphoreType.DMA((spare + 1,))],
        compiler_params=SMALL,
        name="close_high",
    )(exchange(middle), hi_table)
    return closed.reshape(-1, 2, LANES).transpose(1, 0, 2).reshape(stem.shape)


def body(stems, lo_table, hi_table, slice_bits):
    total = one_slice(stems[0], slice_bits[:1], lo_table, hi_table)
    for s in range(1, stems.shape[0]):
        total = total + one_slice(stems[s], slice_bits[s : s + 1], lo_table, hi_table)
    return total


def solution(mesh):
    placed = (P("groups", None, "stem"), P(), P(), P("groups", None))
    return jax.shard_map(
        body, mesh=mesh, in_specs=placed, out_specs=P(None, ("groups", "stem")), check_vma=False
    )
```
